32 devices in a mesh: prompt: 2 (over y), wide: 16 (over z, x, core).
Axes of the slice: x: 2, y: 2, z: 4, core: 2. Of those that a mesh axis runs over, the one named last changes fastest.
Arguments:
- candidate_hidden: bfloat16 [2, 2048, 4096], P('prompt', 'wide'), may hold values from -6 to 6
- frozen_query: bfloat16 [2, 2048, 4096], P('prompt', 'wide'), may hold values from -12 to 12
- candidate_key_value: bfloat16 [2, 2048, 2048], P('prompt', 'wide'), may hold values from -6 to 6
- prompt_key_value: bfloat16 [2, 1024, 2048], P('prompt', 'wide'), may hold values from -12 to 12
- candidate_adapter: int32 [2, 16], P('prompt'), may hold values from 0 to 15
- prompt_block_end: int32 [2, 16], P('prompt', 'wide'), may hold values from 1 to 8, as said below
- adapter_down: bfloat16 [16, 4, 16, 4096], P(None, None, None, 'wide'), may hold values from -0.09375 to 0.09375
- adapter_up: bfloat16 [16, 2, 16, 4096], P(None, None, None, 'wide'), may hold values from -0.625 to 0.625
- adapter_up_key_value: bfloat16 [16, 2, 16, 1024], P(None, None, None, 'wide'), may hold values from -0.625 to 0.625
- output_cotangent: bfloat16 [2, 2048, 4096], P('prompt', 'wide'), may hold values from -0.03125 to 0.03125
- context_cotangent: bfloat16 [2, 2048, 4096], P('prompt', 'wide'), may hold values from -0.03125 to 0.03125
Outputs:
- down_gradient: float32 [16, 4, 16, 4096], P(None, None, None, 'wide')
- up_gradient: float32 [16, 2, 16, 4096], P(None, None, None, 'wide')
- key_value_up_gradient: float32 [16, 2, 16, 1024], P(None, None, None, 'wide')
The draws below stay inside these ranges and needn't reach their ends.
Inputs may be any that keep to these rules, and one draw needn't show every extreme that they name: `prompt_block_end`: the first block of every group sees the whole prompt.
All inputs are finite; a program needn't handle non-finite values.
Results may differ from the reference program's by a relative error of at most 0.02.
Values may be sent and summed in bfloat16 or wider, within the bound.
A program may use at most 192 MiB of HBM per device.

```python
import jax
import jax.numpy as jnp
from jax import lax

MODEL_WIDTH = 4096
HEADS = 32
KV_HEADS = 8
HEAD_DIM = 128
ADAPTER_RANK = 16
ADAPTER_COUNT = 16
BLOCK_TOKENS = 128
KEY_VALUE_WIDTH = 1024
GROUPS = 2
CBLK = 16
CROWS = 2048
PROMPT_LEN = 1024
PBLOCKS = 8


def draw_prompt_key_value(key, part):
    noise = jnp.clip(jax.random.normal(jax.random.fold_in(key, 11), (GROUPS, PROMPT_LEN, 2 * KV_HEADS * HEAD_DIM), jnp.float32), -6.0, 6.0)
    return noise.astype(jnp.bfloat16)


def draw_frozen_query(key, part):
    noise = jnp.clip(jax.random.normal(jax.random.fold_in(key, 21), (GROUPS, CROWS, HEADS * HEAD_DIM), jnp.float32), -6.0, 6.0)
    return noise.astype(jnp.bfloat16)


def draw_prompt_block_end(key, part):
    ends = jax.random.randint(jax.random.fold_in(key, 31), (GROUPS, CBLK), 1, PBLOCKS + 1)
    return ends.at[:, 0].set(PBLOCKS).astype(jnp.int32)


def place_ends(values, key, low, top_value):
    dims = values.shape
    spot = [jax.random.randint(jax.random.fold_in(key, axis), (), 0, dims[axis]) for axis in range(len(dims))]
    values = values.at[tuple(spot)].set(low)
    longest = dims.index(max(dims))
    spot[longest] = (spot[longest] + 1) % dims[longest]
    return values.at[tuple(spot)].set(top_value)


def steps_of(key, shape, pieces, smallest, high):
    factor_of, own = 1.0, jax.random.fold_in(key, 6)
    for position, shards_of in pieces:
        heights = jnp.exp(jax.random.uniform(jax.random.fold_in(own, position), (shards_of,), jnp.float32, smallest / len(pieces), high / len(pieces)))
        factor_of = factor_of * jnp.repeat(heights, shape[position] // shards_of).reshape([-1 if axis == position else 1 for axis in range(len(shape))])
    return factor_of


def centred(rng, shape, width, reach, split=(), held_as=jnp.bfloat16):
    values = width * jax.random.normal(rng, shape, jnp.float32)
    if split:
        values = values * steps_of(rng, shape, split, -0.22, 0.18)
    return jnp.clip(values, -reach, reach).astype(held_as)


def setup_inputs(seed: int = 0) -> dict:
    arg_keys = jax.random.split(jax.random.key(seed), 12)
    return {
        "candidate_hidden": centred(arg_keys[0], (GROUPS, CROWS, MODEL_WIDTH), 1.0, 6.0, ((0, 2), (1, 16))),
        "frozen_query": draw_frozen_query(jax.random.fold_in(arg_keys[11], 71), 0),
        "candidate_key_value": centred(arg_keys[2], (GROUPS, CROWS, 2 * KEY_VALUE_WIDTH), 1.0, 6.0, ((0, 2), (1, 16))),
        "prompt_key_value": draw_prompt_key_value(jax.random.fold_in(arg_keys[11], 71), 0),
        "candidate_adapter": place_ends(jax.random.randint(arg_keys[4], (GROUPS, CBLK), 0, ADAPTER_COUNT), jax.random.fold_in(arg_keys[4], 1), 0, ADAPTER_COUNT - 1).astype(jnp.int32),
        "prompt_block_end": draw_prompt_block_end(jax.random.fold_in(arg_keys[11], 71), 0),
        "adapter_down": centred(arg_keys[6], (ADAPTER_COUNT, 4, ADAPTER_RANK, MODEL_WIDTH), MODEL_WIDTH ** -0.5, 0.09375, ((3, 16),)),
        "adapter_up": centred(arg_keys[7], (ADAPTER_COUNT, 2, ADAPTER_RANK, MODEL_WIDTH), 0.1, 0.625, ((3, 16),)),
        "adapter_up_key_value": centred(arg_keys[8], (ADAPTER_COUNT, 2, ADAPTER_RANK, KEY_VALUE_WIDTH), 0.1, 0.625, ((3, 16),)),
        "output_cotangent": centred(arg_keys[9], (GROUPS, CROWS, MODEL_WIDTH), 0.005, 0.03125, ((0, 2), (1, 16))),
        "context_cotangent": centred(arg_keys[10], (GROUPS, CROWS, MODEL_WIDTH), 0.005, 0.03125, ((0, 2), (1, 16))),
    }


adapter_scale = 2.0
masked_score = -1.0e30


def rounded_input(value):
    return lax.optimization_barrier(value.astype(jnp.bfloat16)).astype(jnp.float32)


def split_heads(rows):
    return rows.reshape(rows.shape[0], KV_HEADS, HEADS // KV_HEADS, HEAD_DIM)


def per_block_gradients(hidden_rows, candidate_query_rows, key_value_rows, output_gradients, context_gradients, adapter_index, last_prompt_block, prompt_token_rows, adapter_down, adapter_up, adapter_up_key_value):
    key_value_width = KV_HEADS * HEAD_DIM
    inverse_root = HEAD_DIM ** -0.5
    down_matrices = adapter_down[adapter_index].astype(jnp.float32)
    up_model_matrix = adapter_up[adapter_index].astype(jnp.float32)
    up_matrix_pairs = adapter_up_key_value[adapter_index].astype(jnp.float32)
    x_wide = hidden_rows.astype(jnp.float32)
    rank_projection = rounded_input(jnp.einsum('bd,prd->prb', x_wide, down_matrices[:3]))
    query_vectors = rounded_input(candidate_query_rows.astype(jnp.float32) + adapter_scale * jnp.einsum('hc,hp->cp', rank_projection[0], up_model_matrix[0]))
    key_value_delta = jnp.einsum('prb,prd->bpd', rank_projection[1:], up_matrix_pairs).reshape(BLOCK_TOKENS, 2 * key_value_width)
    candidate_own_key_value = rounded_input(key_value_rows.astype(jnp.float32) + adapter_scale * key_value_delta)
    prompt_wide = prompt_token_rows.astype(jnp.float32)
    key_rows = jnp.concatenate([prompt_wide[:, :key_value_width], candidate_own_key_value[:, :key_value_width]], axis=0)
    value_rows = jnp.concatenate([prompt_wide[:, key_value_width:], candidate_own_key_value[:, key_value_width:]], axis=0)
    prompt_len = prompt_token_rows.shape[0]
    prompt_seen = jnp.arange(prompt_len)[None, :] < last_prompt_block * BLOCK_TOKENS
    causal = jnp.arange(BLOCK_TOKENS)[None, :] <= jnp.arange(BLOCK_TOKENS)[:, None]
    visible = jnp.concatenate([jnp.broadcast_to(prompt_seen, (BLOCK_TOKENS, prompt_len)), causal], axis=1)
    query_heads = split_heads(query_vectors)
    key_heads = key_rows.reshape(-1, KV_HEADS, HEAD_DIM)
    value_heads = value_rows.reshape(-1, KV_HEADS, HEAD_DIM)
    scores = jnp.where(visible, jnp.einsum('bkgd,jkd->kgbj', query_heads, key_heads) * inverse_root, masked_score)
    row_peak = jnp.max(scores, axis=-1, keepdims=True)
    exponent = jnp.where(visible, jnp.exp(scores - row_peak), 0.0)
    row_total = jnp.sum(exponent, axis=-1)
    weighted = jnp.einsum('kgbj,jkd->bkgd', rounded_input(exponent), value_heads)
    context = rounded_input(weighted / jnp.transpose(row_total, (2, 0, 1))[..., None]).reshape(BLOCK_TOKENS, HEADS * HEAD_DIM)
    output_model_rows = output_gradients.astype(jnp.float32)
    output_rank_rows = rounded_input(jnp.einsum('ae,me->ma', context, down_matrices[3]))
    up_gradient_result = adapter_scale * jnp.einsum('su,ui->si', output_rank_rows, output_model_rows)
    up_output_matrix = rounded_input(adapter_scale * jnp.einsum('ae,me->ma', output_model_rows, up_model_matrix[1]))
    grad_a_out = jnp.einsum('su,ui->si', up_output_matrix, context)
    context_grad = rounded_input(context_gradients.astype(jnp.float32) + jnp.einsum('hc,hp->cp', up_output_matrix, down_matrices[3]))
    grad_heads = split_heads(context_grad)
    row_delta = jnp.transpose(jnp.sum(grad_heads * split_heads(context), axis=-1), (1, 2, 0))
    attention = exponent / row_total[..., None]
    attention_grad = jnp.einsum('bkgd,jkd->kgbj', grad_heads, value_heads)
    score_grad = rounded_input(attention * (attention_grad - row_delta[..., None]))
    query_gradient = rounded_input(jnp.einsum('kgbj,jkd->bkgd', score_grad, key_heads) * inverse_root).reshape(BLOCK_TOKENS, HEADS * HEAD_DIM)
    key_grad = jnp.einsum('kgbj,bkgd->jkd', score_grad[..., prompt_len:], query_heads) * inverse_root
    value_grad = jnp.einsum('kgbj,bkgd->jkd', rounded_input(attention[..., prompt_len:]), grad_heads)
    key_value_gradient = rounded_input(jnp.stack([key_grad.reshape(BLOCK_TOKENS, key_value_width), value_grad.reshape(BLOCK_TOKENS, key_value_width)], axis=1))
    up_query_matrix = rounded_input(adapter_scale * jnp.einsum('ae,me->ma', query_gradient, up_model_matrix[0]))
    up_rank_key_value = rounded_input(adapter_scale * jnp.einsum('ztf,tkf->tkz', key_value_gradient, up_matrix_pairs))
    grad_a_qkv = jnp.einsum('prb,bd->prd', jnp.concatenate([up_query_matrix[None], up_rank_key_value], axis=0), x_wide)
    down_gradient = jnp.concatenate([grad_a_qkv, grad_a_out[None]], axis=0)
    up_gradient = jnp.stack([adapter_scale * jnp.einsum('su,ui->si', rank_projection[0], query_gradient), up_gradient_result], axis=0)
    key_value_up_gradient = adapter_scale * jnp.einsum('yzm,myk->yzk', rank_projection[1:], key_value_gradient)
    return down_gradient, up_gradient, key_value_up_gradient


def reference(candidate_hidden, frozen_query, candidate_key_value, prompt_key_value, candidate_adapter, prompt_block_end, adapter_down, adapter_up, adapter_up_key_value, output_cotangent, context_cotangent):
    block_count = GROUPS * CBLK
    block_items = (
        candidate_hidden.reshape(block_count, BLOCK_TOKENS, -1),
        frozen_query.reshape(block_count, BLOCK_TOKENS, -1),
        candidate_key_value.reshape(block_count, BLOCK_TOKENS, -1),
        output_cotangent.reshape(block_count, BLOCK_TOKENS, -1),
        context_cotangent.reshape(block_count, BLOCK_TOKENS, -1),
        candidate_adapter.reshape(block_count).astype(jnp.int32),
        prompt_block_end.reshape(block_count).astype(jnp.int32),
        (jnp.arange(block_count) // CBLK).astype(jnp.int32),
    )

    def accumulate(running, item_now):
        hidden_rows, candidate_query_rows, key_value_rows, output_gradients, context_gradients, adapter_index, last_prompt_block, group_index = item_now
        prompt_token_rows = lax.dynamic_index_in_dim(prompt_key_value, group_index, 0, keepdims=False)
        down_gradient, up_gradient, key_value_up_gradient = per_block_gradients(hidden_rows, candidate_query_rows, key_value_rows, output_gradients, context_gradients, adapter_index, last_prompt_block, prompt_token_rows, adapter_down, adapter_up, adapter_up_key_value)
        return (running[0].at[adapter_index].add(down_gradient), running[1].at[adapter_index].add(up_gradient), running[2].at[adapter_index].add(key_value_up_gradient)), None

    start_state = (
        jnp.zeros(adapter_down.shape, jnp.float32),
        jnp.zeros(adapter_up.shape, jnp.float32),
        jnp.zeros(adapter_up_key_value.shape, jnp.float32),
    )
    totals, _ = lax.scan(accumulate, start_state, block_items)
    return totals[0], totals[1], totals[2]
```

```python
import functools

import jax
import jax.numpy as jnp
from jax import lax
from jax.experimental import pallas as pl
from jax.experimental.pallas import tpu as pltpu
from jax.sharding import PartitionSpec as P

HEADS = 32
KV_HEADS = 8
HEAD_DIM = 128
ADAPTER_COUNT = 16
BLOCK_TOKENS = 128
RANK = 16
HEAD_GROUP = HEADS // KV_HEADS
GROUP_WIDTH = HEAD_GROUP * HEAD_DIM
MESH = pl.DeviceIdType.MESH

adapter_scale = 2.0
masked_score = -1e30
LOG2E = 1.4426950408889634


def dot(a, b, contract=((1,), (0,))):
    return lax.dot_general(a, b, (contract, ((), ())), preferred_element_type=jnp.float32)


NT = ((1,), (1,))
TN = ((0,), (0,))


def chip_at(place, chips):
    place = lax.rem(place + chips, chips)
    return jnp.where(place < chips // 2, 2 * place, 2 * (chips - 1 - place) + 1)


def gather_kernel(n, send_ref, send_pair_ref, prompt_ref, maps_ref, pairs_ref, rows_ref,
                  local_sem, ring_send, ring_recv, core_send, core_recv, part_send, part_recv):
    p = lax.axis_index("prompt")
    w = lax.axis_index("wide")
    chips = n // 2
    half = chips // 2
    core = lax.rem(w, 2)
    chip = w // 2
    place = jnp.where(lax.rem(chip, 2) == 0, chip // 2, chips - 1 - chip // 2)
    rows = prompt_ref.shape[0]
    columns = send_ref.shape[2]
    partner = w + 1 - 2 * core
    ahead = 2 * chip_at(place + 1, chips) + core
    behind = 2 * chip_at(place - 1, chips) + core

    barrier = pltpu.get_barrier_semaphore()
    for k in range(1, n):
        pl.semaphore_signal(barrier, inc=1, device_id=(p, lax.rem(w + k, n)), device_id_type=MESH)
    pl.semaphore_wait(barrier, n - 1)

    def shard(offset):
        return 2 * chip_at(place + offset, chips) + core

    def remote(src, dst, send, recv, to):
        copy = pltpu.make_async_remote_copy(
            src_ref=src, dst_ref=dst, send_sem=send, recv_sem=recv, device_id=(p, to), device_id_type=MESH
        )
        copy.start()
        return copy

    def window(owner, start, size):
        return rows_ref.at[pl.ds(pl.multiple_of(owner * rows + start, 16), size), :]

    sent = []
    cut = rows // 2
    ring = {}

    def pass_on(direction, step, source, owner):
        to = ahead if direction == 0 else behind
        if step < half:
            start, size = 0, rows
        else:
            start, size = (0, cut) if direction == 0 else (cut, rows - cut)
        if source is None:
            src = window(owner, start, size)
        else:
            src = source.at[pl.ds(start, size), :]
        ring[direction, step] = remote(
            src, window(owner, start, size), ring_send.at[direction, step], ring_recv.at[direction, step], to
        )

    pass_on(0, 1, prompt_ref, w)
    pass_on(1, 1, prompt_ref, w)
    sent.append(remote(prompt_ref, window(w, 0, rows), core_send.at[0], core_recv.at[0], partner))
    locals_ = [
        pltpu.make_async_copy(prompt_ref, window(w, 0, rows), local_sem.at[0]),
        pltpu.make_async_copy(
            send_ref.at[w], maps_ref.at[:, pl.ds(pl.multiple_of(w * columns, 128), columns)], local_sem.at[1]
        ),
        pltpu.make_async_copy(send_pair_ref.at[w], pairs_ref.at[w], local_sem.at[2]),
    ]
    for copy in locals_:
        copy.start()
    parts = []
    for k in range(1, n):
        to = lax.rem(w + k, n)
        parts.append(
            remote(
                send_ref.at[to],
                maps_ref.at[:, pl.ds(pl.multiple_of(w * columns, 128), columns)],
                part_send.at[0, k], part_recv.at[0, k], to,
            )
        )
        parts.append(
            remote(send_pair_ref.at[to], pairs_ref.at[w], part_send.at[1, k], part_recv.at[1, k], to)
        )
    slot = 1
    for step in range(1, half + 1):
        from_behind, from_ahead = shard(-step), shard(step)
        ring[0, step].wait_recv()
        if step < half:
            pass_on(0, step + 1, None, from_behind)
        ring[1, step].wait_recv()
        if step < half:
            pass_on(1, step + 1, None, from_ahead)
        arrived = (from_behind, from_ahead) if step < half else (from_behind,)
        for owner in arrived:
            here = window(owner, 0, rows)
            sent.append(remote(here, here, core_send.at[slot], core_recv.at[slot], partner))
            slot += 1
    for copy in ring.values():
        copy.wait_send()
    for copy in sent:
        copy.wait_send()
        copy.wait_recv()
    for copy in parts:
        copy.wait_send()
        copy.wait_recv()
    for copy in locals_:
        copy.wait()


def gather(n, send, send_pair, prompt_rows):
    _, map_rows, columns = send.shape
    rows, width = prompt_rows.shape
    chips = n // 2
    half = chips // 2
    any_spec = pl.BlockSpec(memory_space=pl.ANY)
    return pl.pallas_call(
        functools.partial(gather_kernel, n),
        out_shape=(
            jax.ShapeDtypeStruct((map_rows, n * columns), jnp.bfloat16),
            jax.ShapeDtypeStruct(send_pair.shape, jnp.bfloat16),
            jax.ShapeDtypeStruct((n * rows, width), jnp.bfloat16),
        ),
        in_specs=[any_spec] * 3,
        out_specs=(any_spec,) * 3,
        scratch_shapes=[
            pltpu.SemaphoreType.DMA((3,)),
            pltpu.SemaphoreType.DMA((2, half + 1)),
            pltpu.SemaphoreType.DMA((2, half + 1)),
            pltpu.SemaphoreType.DMA((chips,)),
            pltpu.SemaphoreType.DMA((chips,)),
            pltpu.SemaphoreType.DMA((2, n)),
            pltpu.SemaphoreType.DMA((2, n)),
        ],
        compiler_params=pltpu.CompilerParams(collective_id=0, has_side_effects=True),
    )(send, send_pair, prompt_rows)


def spread_kernel(groups, n, maps_ref, pairs_ref, back_ref, back_pair_ref,
                  local_sem, part_send, part_recv, far_send, far_recv):
    p = lax.axis_index("prompt")
    w = lax.axis_index("wide")
    columns = back_ref.shape[3]

    barrier = pltpu.get_barrier_semaphore()
    for k in range(1, n):
        pl.semaphore_signal(barrier, inc=1, device_id=(p, lax.rem(w + k, n)), device_id_type=MESH)
    for k in range(1, groups):
        pl.semaphore_signal(barrier, inc=1, device_id=(lax.rem(p + k, groups), w), device_id_type=MESH)
    pl.semaphore_wait(barrier, n + groups - 2)

    def remote(src, dst, send, recv, to):
        copy = pltpu.make_async_remote_copy(
            src_ref=src, dst_ref=dst, send_sem=send, recv_sem=recv, device_id=to, device_id_type=MESH
        )
        copy.start()
        return copy

    def mine(to):
        return maps_ref.at[:, pl.ds(pl.multiple_of(to * columns, 128), columns)]

    locals_ = [
        pltpu.make_async_copy(mine(w), back_ref.at[p, w], local_sem.at[0]),
        pltpu.make_async_copy(pairs_ref.at[w], back_pair_ref.at[p, w], local_sem.at[1]),
    ]
    for copy in locals_:
        copy.start()
    parts = []
    for k in range(1, n):
        to = lax.rem(w + k, n)
        parts.append((
            remote(mine(to), back_ref.at[p, w], part_send.at[0, k], part_recv.at[0, k], (p, to)),
            remote(pairs_ref.at[to], back_pair_ref.at[p, w], part_send.at[1, k], part_recv.at[1, k], (p, to)),
        ))
    far = []

    def pass_on(owner, slot, source, source_pair):
        for k in range(1, groups):
            to = (lax.rem(p + k, groups), w)
            far.append(
                remote(source, back_ref.at[p, owner], far_send.at[0, k, slot], far_recv.at[0, k, slot], to)
            )
            far.append(
                remote(source_pair, back_pair_ref.at[p, owner], far_send.at[1, k, slot], far_recv.at[1, k, slot], to)
            )

    pass_on(w, 0, mine(w), pairs_ref.at[w])
    for k in range(1, n):
        owner = lax.rem(w - k + n, n)
        parts[k - 1][0].wait_recv()
        parts[k - 1][1].wait_recv()
        pass_on(owner, k, back_ref.at[p, owner], back_pair_ref.at[p, owner])
    for pair in parts:
        for copy in pair:
            copy.wait_send()
    for copy in far:
        copy.wait_send()
        copy.wait_recv()
    for copy in locals_:
        copy.wait()


def spread(groups, n, maps, pairs):
    map_rows, width = maps.shape
    columns = width // n
    any_spec = pl.BlockSpec(memory_space=pl.ANY)
    return pl.pallas_call(
        functools.partial(spread_kernel, groups, n),
        out_shape=(
            jax.ShapeDtypeStruct((groups, n, map_rows, columns), jnp.bfloat16),
            jax.ShapeDtypeStruct((groups,) + pairs.shape, jnp.bfloat16),
        ),
        in_specs=[any_spec] * 2,
        out_specs=(any_spec,) * 2,
        scratch_shapes=[
            pltpu.SemaphoreType.DMA((2,)),
            pltpu.SemaphoreType.DMA((2, n)),
            pltpu.SemaphoreType.DMA((2, n)),
            pltpu.SemaphoreType.DMA((2, groups, n)),
            pltpu.SemaphoreType.DMA((2, groups, n)),
        ],
        compiler_params=pltpu.CompilerParams(collective_id=1, has_side_effects=True),
    )(maps, pairs)


def block_kernel(end_ref, x_ref, query_ref, own_key_ref, own_value_ref, key_ref, value_ref, maps_ref,
                 pairs_ref, cotangent_ref, context_cotangent_ref, grads_ref, pair_grads_ref,
                 low_t, low, up_out, up_out_t, sums):
    head = pl.program_id(0)
    inverse_root = HEAD_DIM ** (-0.5)
    pair_columns = pairs_ref.shape[2]
    pieces = HEAD_DIM // pair_columns
    prompt_len = key_ref.shape[0]

    @pl.when(head == 0)
    def _():
        x = x_ref[...]
        low_t[...] = dot(x, maps_ref[0:48, :], NT).astype(jnp.bfloat16)
        low[...] = dot(maps_ref[0:48, :], x, NT).astype(jnp.bfloat16)
        up_out_t[...] = (adapter_scale * dot(cotangent_ref[...], maps_ref[80:96, :], NT)).astype(jnp.bfloat16)
        up_out[...] = (adapter_scale * dot(maps_ref[80:96, :], cotangent_ref[...], NT)).astype(jnp.bfloat16)
        sums[...] = jnp.zeros_like(sums)

    columns = pl.ds(pl.multiple_of(head * GROUP_WIDTH, GROUP_WIDTH), GROUP_WIDTH)
    down_out = maps_ref[48:64, columns]
    up_query = maps_ref[64:80, columns]
    up_pair = jnp.concatenate([pairs_ref[head * pieces + i] for i in range(pieces)], axis=1)

    queries = (
        query_ref[...].astype(jnp.float32) + adapter_scale * dot(low_t[:, 0:16], up_query)
    ).astype(jnp.bfloat16)
    own_key = (
        own_key_ref[...].astype(jnp.float32) + adapter_scale * dot(low_t[:, 16:32], up_pair[0:16])
    ).astype(jnp.bfloat16)
    own_value = (
        own_value_ref[...].astype(jnp.float32) + adapter_scale * dot(low_t[:, 32:48], up_pair[16:32])
    ).astype(jnp.bfloat16)
    context_grad = (
        context_cotangent_ref[...].astype(jnp.float32) + dot(up_out_t[...], down_out)
    ).astype(jnp.bfloat16)

    limit = end_ref[0, 0] * BLOCK_TOKENS
    prompt_bias = jnp.where(
        lax.broadcasted_iota(jnp.int32, (1, prompt_len), 1) < limit, 0.0, masked_score
    )
    together = 2
    row = lax.broadcasted_iota(jnp.int32, (together * BLOCK_TOKENS, BLOCK_TOKENS), 0) % BLOCK_TOKENS
    column = lax.broadcasted_iota(jnp.int32, (together * BLOCK_TOKENS, BLOCK_TOKENS), 1)
    own_bias = jnp.where(column <= row, 0.0, masked_score)

    def stack(array, first):
        return jnp.concatenate(
            [array[:, (first + i) * HEAD_DIM:(first + i + 1) * HEAD_DIM] for i in range(together)], axis=0
        )

    def side(array):
        return [array[i * BLOCK_TOKENS:(i + 1) * BLOCK_TOKENS] for i in range(together)]

    keys = key_ref[...]
    values = value_ref[...]
    contexts, query_grads = [], []
    key_grad = jnp.zeros((BLOCK_TOKENS, HEAD_DIM), jnp.float32)
    value_grad = jnp.zeros((BLOCK_TOKENS, HEAD_DIM), jnp.float32)
    for first in range(0, HEAD_GROUP, together):
        q = stack(queries, first)
        g = stack(context_grad, first)
        scores = dot(q, keys, NT) + prompt_bias
        own_scores = dot(q, own_key, NT) + own_bias
        peak = jnp.maximum(
            jnp.max(scores, axis=1, keepdims=True), jnp.max(own_scores, axis=1, keepdims=True)
        )
        exponent = jnp.exp2((scores - peak) * (inverse_root * LOG2E))
        own_exponent = jnp.exp2((own_scores - peak) * (inverse_root * LOG2E))
        total = jnp.sum(exponent, axis=1, keepdims=True) + jnp.sum(own_exponent, axis=1, keepdims=True)
        share = 1.0 / total
        weighted = dot(exponent.astype(jnp.bfloat16), values) + dot(own_exponent.astype(jnp.bfloat16), own_value)
        context = (weighted * share).astype(jnp.bfloat16)
        delta = jnp.sum(g.astype(jnp.float32) * context.astype(jnp.float32), axis=1, keepdims=True)
        score_grad = (exponent * share * (dot(g, values, NT) - delta)).astype(jnp.bfloat16)
        own_attention = own_exponent * share
        own_score_grad = (own_attention * (dot(g, own_value, NT) - delta)).astype(jnp.bfloat16)
        query_grad = ((dot(score_grad, keys) + dot(own_score_grad, own_key)) * inverse_root).astype(jnp.bfloat16)
        key_grad += dot(own_score_grad, q, TN)
        value_grad += dot(own_attention.astype(jnp.bfloat16), g, TN)
        contexts += side(context)
        query_grads += side(query_grad)
    context = jnp.concatenate(contexts, axis=1)
    query_grad = jnp.concatenate(query_grads, axis=1)
    key_grad = (key_grad * inverse_root).astype(jnp.bfloat16)
    value_grad = value_grad.astype(jnp.bfloat16)

    sums[0:16, :] += dot(up_query, query_grad, NT)
    sums[16:32, :] += dot(up_pair[0:16], key_grad, NT)
    sums[32:48, :] += dot(up_pair[16:32], value_grad, NT)
    sums[48:64, :] += dot(down_out, context, NT)
    grads_ref[48:64, columns] = dot(up_out[...], context).astype(jnp.bfloat16)
    grads_ref[64:80, columns] = (adapter_scale * dot(low[0:16, :], query_grad)).astype(jnp.bfloat16)
    pair_grad = jnp.concatenate(
        [dot(low[16:32, :], key_grad), dot(low[32:48, :], value_grad)], axis=0
    ) * adapter_scale
    pair_grad = pair_grad.astype(jnp.bfloat16)
    for i in range(pieces):
        pair_grads_ref[head * pieces + i] = pair_grad[:, i * pair_columns:(i + 1) * pair_columns]

    @pl.when(head == KV_HEADS - 1)
    def _():
        up_low = (adapter_scale * sums[0:48, :]).astype(jnp.bfloat16)
        out_low = sums[48:64, :].astype(jnp.bfloat16)
        grads_ref[0:48, :] = dot(up_low, x_ref[...]).astype(jnp.bfloat16)
        grads_ref[80:96, :] = (adapter_scale * dot(out_low, cotangent_ref[...])).astype(jnp.bfloat16)


def block_gradients(end, x, query, own_pair, prompt_rows, maps, pairs, cotangent, context_cotangent):
    tokens, width = x.shape
    prompt_len = prompt_rows.shape[0]

    def whole(array):
        return pl.BlockSpec(array.shape, lambda k: (0,) * array.ndim)

    return pl.pallas_call(
        block_kernel,
        grid=(KV_HEADS,),
        out_shape=(
            jax.ShapeDtypeStruct(maps.shape, jnp.bfloat16),
            jax.ShapeDtypeStruct(pairs.shape, jnp.bfloat16),
        ),
        in_specs=[
            pl.BlockSpec(memory_space=pltpu.SMEM),
            whole(x),
            pl.BlockSpec((tokens, GROUP_WIDTH), lambda k: (0, k)),
            pl.BlockSpec((tokens, HEAD_DIM), lambda k: (0, k)),
            pl.BlockSpec((tokens, HEAD_DIM), lambda k: (0, KV_HEADS + k)),
            pl.BlockSpec((prompt_len, HEAD_DIM), lambda k: (0, k)),
            pl.BlockSpec((prompt_len, HEAD_DIM), lambda k: (0, KV_HEADS + k)),
            whole(maps),
            whole(pairs),
            whole(cotangent),
            pl.BlockSpec((tokens, GROUP_WIDTH), lambda k: (0, k)),
        ],
        out_specs=(whole(maps), whole(pairs)),
        scratch_shapes=[
            pltpu.VMEM((tokens, 48), jnp.bfloat16),
            pltpu.VMEM((48, tokens), jnp.bfloat16),
            pltpu.VMEM((16, tokens), jnp.bfloat16),
            pltpu.VMEM((tokens, 16), jnp.bfloat16),
            pltpu.VMEM((64, tokens), jnp.float32),
        ],
        compiler_params=pltpu.CompilerParams(vmem_limit_bytes=48 * 1024 * 1024),
    )(end, x, query, own_pair, own_pair, prompt_rows, prompt_rows, maps, pairs, cotangent, context_cotangent)


def total_kernel(groups, n, ids_ref, back_ref, back_pair_ref, down_ref, up_ref, pair_ref):
    down_ref[...] = jnp.zeros_like(down_ref)
    up_ref[...] = jnp.zeros_like(up_ref)
    pair_ref[...] = jnp.zeros_like(pair_ref)
    for group in range(groups):
        def step(source, carry):
            adapter = ids_ref[group, source]
            for part in range(4):
                down_ref[adapter, part] += back_ref[group, source, 16 * part:16 * (part + 1)].astype(jnp.float32)
            for part in range(2):
                up_ref[adapter, part] += back_ref[group, source, 64 + 16 * part:80 + 16 * part].astype(jnp.float32)
                pair_ref[adapter, part] += back_pair_ref[group, source, 16 * part:16 * (part + 1)].astype(jnp.float32)
            return carry

        lax.fori_loop(0, n, step, 0)


def totals(ids, back, back_pair):
    groups, n, _, columns = back.shape
    vmem = pl.BlockSpec(memory_space=pltpu.VMEM)
    return pl.pallas_call(
        functools.partial(total_kernel, groups, n),
        out_shape=(
            jax.ShapeDtypeStruct((ADAPTER_COUNT, 4, RANK, columns), jnp.float32),
            jax.ShapeDtypeStruct((ADAPTER_COUNT, 2, RANK, columns), jnp.float32),
            jax.ShapeDtypeStruct((ADAPTER_COUNT, 2, RANK, back_pair.shape[3]), jnp.float32),
        ),
        in_specs=[pl.BlockSpec(memory_space=pltpu.SMEM), vmem, vmem],
        out_specs=(vmem, vmem, vmem),
        compiler_params=pltpu.CompilerParams(vmem_limit_bytes=48 * 1024 * 1024),
    )(ids, back, back_pair)


def body(
    groups, n,
    candidate_hidden,
    frozen_query,
    candidate_key_value,
    prompt_key_value,
    candidate_adapter,
    prompt_block_end,
    adapter_down,
    adapter_up,
    adapter_up_key_value,
    output_cotangent,
    context_cotangent,
):
    ids = candidate_adapter[0]
    columns = adapter_down.shape[3]
    all_ids = lax.all_gather(ids, "prompt", axis=0)
    send = jnp.concatenate(
        [adapter_down[ids].reshape(n, 4 * RANK, columns), adapter_up[ids].reshape(n, 2 * RANK, columns)], axis=1
    )
    send_pair = adapter_up_key_value[ids].reshape(n, 2 * RANK, adapter_up_key_value.shape[3])
    maps, pairs, prompt_rows = gather(n, send, send_pair, prompt_key_value[0])
    grads, pair_grads = block_gradients(
        prompt_block_end, candidate_hidden[0], frozen_query[0], candidate_key_value[0], prompt_rows,
        maps, pairs, output_cotangent[0], context_cotangent[0],
    )
    back, back_pair = spread(groups, n, grads, pair_grads)
    return totals(all_ids, back, back_pair)


def solution(mesh):
    placed = (
        P("prompt", "wide", None),
        P("prompt", "wide", None),
        P("prompt", "wide", None),
        P("prompt", "wide", None),
        P("prompt", None),
        P("prompt", "wide"),
        P(None, None, None, "wide"),
        P(None, None, None, "wide"),
        P(None, None, None, "wide"),
        P("prompt", "wide", None),
        P("prompt", "wide", None),
    )
    return jax.shard_map(
        functools.partial(body, mesh.shape["prompt"], mesh.shape["wide"]),
        mesh=mesh,
        in_specs=placed,
        out_specs=(
            P(None, None, None, "wide"),
            P(None, None, None, "wide"),
            P(None, None, None, "wide"),
        ),
        check_vma=False,
    )
```

```python
import functools

import jax
import jax.numpy as jnp
from jax import lax
from jax.experimental import pallas as pl
from jax.experimental.pallas import tpu as pltpu
from jax.sharding import PartitionSpec as P

HEADS = 32
KV_HEADS = 8
HEAD_DIM = 128
ADAPTER_COUNT = 16
BLOCK_TOKENS = 128
RANK = 16
HEAD_GROUP = HEADS // KV_HEADS
GROUP_WIDTH = HEAD_GROUP * HEAD_DIM
MESH = pl.DeviceIdType.MESH

adapter_scale = 2.0
masked_score = -1e30
LOG2E = 1.4426950408889634


def dot(a, b, contract=((1,), (0,))):
    return lax.dot_general(a, b, (contract, ((), ())), preferred_element_type=jnp.float32)


NT = ((1,), (1,))
TN = ((0,), (0,))


def chip_at(place, chips):
    place = lax.rem(place + chips, chips)
    return jnp.where(place < chips // 2, 2 * place, 2 * (chips - 1 - place) + 1)


def spread_kernel(groups, n, maps_ref, pairs_ref, ids_ref, back_ref, back_pair_ref, all_ids_ref,
                  local_sem, part_send, part_recv, far_send, far_recv, ids_send, ids_recv):
    p = lax.axis_index("prompt")
    w = lax.axis_index("wide")
    columns = back_ref.shape[3]

    barrier = pltpu.get_barrier_semaphore()
    for k in range(1, n):
        pl.semaphore_signal(barrier, inc=1, device_id=(p, lax.rem(w + k, n)), device_id_type=MESH)
    for k in range(1, groups):
        pl.semaphore_signal(barrier, inc=1, device_id=(lax.rem(p + k, groups), w), device_id_type=MESH)
    pl.semaphore_wait(barrier, n + groups - 2)

    def remote(src, dst, send, recv, to):
        copy = pltpu.make_async_remote_copy(
            src_ref=src, dst_ref=dst, send_sem=send, recv_sem=recv, device_id=to, device_id_type=MESH
        )
        copy.start()
        return copy

    def mine(to):
        return maps_ref.at[:, pl.ds(pl.multiple_of(to * columns, 128), columns)]

    locals_ = [
        pltpu.make_async_copy(mine(w), back_ref.at[p, w], local_sem.at[0]),
        pltpu.make_async_copy(pairs_ref.at[w], back_pair_ref.at[p, w], local_sem.at[1]),
        pltpu.make_async_copy(ids_ref, all_ids_ref.at[p], local_sem.at[2]),
    ]
    for copy in locals_:
        copy.start()
    parts = []
    for k in range(1, n):
        to = lax.rem(w + k, n)
        parts.append((
            remote(mine(to), back_ref.at[p, w], part_send.at[0, k], part_recv.at[0, k], (p, to)),
            remote(pairs_ref.at[to], back_pair_ref.at[p, w], part_send.at[1, k], part_recv.at[1, k], (p, to)),
        ))
    far = [
        remote(ids_ref, all_ids_ref.at[p], ids_send.at[k], ids_recv.at[k], (lax.rem(p + k, groups), w))
        for k in range(1, groups)
    ]

    def pass_on(owner, slot, source, source_pair):
        for k in range(1, groups):
            to = (lax.rem(p + k, groups), w)
            far.append(
                remote(source, back_ref.at[p, owner], far_send.at[0, k, slot], far_recv.at[0, k, slot], to)
            )
            far.append(
                remote(source_pair, back_pair_ref.at[p, owner], far_send.at[1, k, slot], far_recv.at[1, k, slot], to)
            )

    pass_on(w, 0, mine(w), pairs_ref.at[w])
    for k in range(1, n):
        owner = lax.rem(w - k + n, n)
        parts[k - 1][0].wait_recv()
        parts[k - 1][1].wait_recv()
        pass_on(owner, k, back_ref.at[p, owner], back_pair_ref.at[p, owner])
    for pair in parts:
        for copy in pair:
            copy.wait_send()
    for copy in far:
        copy.wait_send()
        copy.wait_recv()
    for copy in locals_:
        copy.wait()


def spread(groups, n, maps, pairs, ids):
    map_rows, width = maps.shape
    columns = width // n
    any_spec = pl.BlockSpec(memory_space=pl.ANY)
    return pl.pallas_call(
        functools.partial(spread_kernel, groups, n),
        out_shape=(
            jax.ShapeDtypeStruct((groups, n, map_rows, columns), jnp.bfloat16),
            jax.ShapeDtypeStruct((groups,) + pairs.shape, jnp.bfloat16),
            jax.ShapeDtypeStruct((groups,) + ids.shape, jnp.int32),
        ),
        in_specs=[any_spec] * 3,
        out_specs=(any_spec,) * 3,
        scratch_shapes=[
            pltpu.SemaphoreType.DMA((3,)),
            pltpu.SemaphoreType.DMA((2, n)),
            pltpu.SemaphoreType.DMA((2, n)),
            pltpu.SemaphoreType.DMA((2, groups, n)),
            pltpu.SemaphoreType.DMA((2, groups, n)),
            pltpu.SemaphoreType.DMA((groups,)),
            pltpu.SemaphoreType.DMA((groups,)),
        ],
        compiler_params=pltpu.CompilerParams(collective_id=1, has_side_effects=True),
    )(maps, pairs, ids)


PIECES = 4
PIECE_HEADS = KV_HEADS // PIECES
PIECE_WIDTH = PIECE_HEADS * HEAD_DIM


def block_kernel(n, end_ref, x_ref, query_ref, own_ref, cotangent_ref, context_cotangent_ref,
                 send_down_ref, send_up_ref, send_pair_ref, prompt_ref, grads_ref, pair_grads_ref,
                 maps_ref, pairs_ref, rows_ref, low_t, low, up_out, up_out_t, sums,
                 local_sem, own_sem, ring_send, ring_recv, core_send, core_recv, part_send, part_recv):
    p = lax.axis_index("prompt")
    w = lax.axis_index("wide")
    chips = n // 2
    half = chips // 2
    core = lax.rem(w, 2)
    chip = w // 2
    place = jnp.where(lax.rem(chip, 2) == 0, chip // 2, chips - 1 - chip // 2)
    rows = prompt_ref.shape[1]
    cut = rows // 2
    map_columns = send_down_ref.shape[2]
    partner = w + 1 - 2 * core
    ahead = 2 * chip_at(place + 1, chips) + core
    behind = 2 * chip_at(place - 1, chips) + core

    barrier = pltpu.get_barrier_semaphore()
    for k in range(1, n):
        pl.semaphore_signal(barrier, inc=1, device_id=(p, lax.rem(w + k, n)), device_id_type=MESH)
    pl.semaphore_wait(barrier, n - 1)

    def shard(offset):
        return 2 * chip_at(place + offset, chips) + core

    def remote(src, dst, send, recv, to):
        return pltpu.make_async_remote_copy(
            src_ref=src, dst_ref=dst, send_sem=send, recv_sem=recv, device_id=(p, to), device_id_type=MESH
        )

    def window(piece, owner, start, size):
        return rows_ref.at[piece, pl.ds(pl.multiple_of(owner * rows + start, 16), size), :]

    def ring(piece, direction, step):
        owner = shard(1 - step) if direction == 0 else shard(step - 1)
        if step < half:
            start, size = 0, rows
        else:
            start, size = (0, cut) if direction == 0 else (cut, rows - cut)
        if step == 1:
            src = prompt_ref.at[piece, pl.ds(start, size), :]
        else:
            src = window(piece, owner, start, size)
        return remote(
            src, window(piece, owner, start, size), ring_send.at[piece, direction, step],
            ring_recv.at[piece, direction, step], ahead if direction == 0 else behind,
        )

    def across(piece, slot):
        if slot == 0:
            src, owner = prompt_ref.at[piece], w
        else:
            step = (slot + 1) // 2
            owner = shard(-step) if slot % 2 == 1 else shard(step)
            src = window(piece, owner, 0, rows)
        return remote(
            src, window(piece, owner, 0, rows), core_send.at[piece, slot], core_recv.at[piece, slot], partner
        )

    def own_copy(piece):
        return pltpu.make_async_copy(prompt_ref.at[piece], window(piece, w, 0, rows), own_sem.at[piece])

    def begin(piece):
        ring(piece, 0, 1).start()
        ring(piece, 1, 1).start()
        across(piece, 0).start()
        own_copy(piece).start()

    def hop(piece, step):
        for direction in range(2):
            ring(piece, direction, step).wait_recv()
            if step < half:
                ring(piece, direction, step + 1).start()
        across(piece, 2 * step - 1).start()
        if step < half:
            across(piece, 2 * step).start()

    part_columns = pl.ds(pl.multiple_of(w * map_columns, 128), map_columns)
    down_here = maps_ref.at[0:64, part_columns]
    up_here = maps_ref.at[64:96, part_columns]
    pair_here = pairs_ref.at[w]
    locals_ = [
        pltpu.make_async_copy(send_down_ref.at[w], down_here, local_sem.at[0]),
        pltpu.make_async_copy(send_up_ref.at[w], up_here, local_sem.at[1]),
        pltpu.make_async_copy(send_pair_ref.at[w], pair_here, local_sem.at[2]),
    ]
    for copy in locals_:
        copy.start()
    parts = []
    for k in range(1, n):
        to = lax.rem(w + k, n)
        for i, (src, dst) in enumerate((
            (send_down_ref.at[to], down_here), (send_up_ref.at[to], up_here), (send_pair_ref.at[to], pair_here)
        )):
            copy = remote(src, dst, part_send.at[i, k], part_recv.at[i, k], to)
            copy.start()
            parts.append(copy)
    begin(0)
    for step in range(1, half + 1):
        hop(0, step)
    begin(1)
    for copy in locals_:
        copy.wait()
    for copy in parts:
        copy.wait_recv()

    inverse_root = HEAD_DIM ** (-0.5)
    pair_columns = pairs_ref.shape[2]
    lanes = HEAD_DIM // pair_columns
    prompt_len = rows_ref.shape[1]

    x = x_ref[...]
    low_t[...] = dot(x, maps_ref[0:48, :], NT).astype(jnp.bfloat16)
    low[...] = dot(maps_ref[0:48, :], x, NT).astype(jnp.bfloat16)
    up_out_t[...] = (adapter_scale * dot(cotangent_ref[...], maps_ref[80:96, :], NT)).astype(jnp.bfloat16)
    up_out[...] = (adapter_scale * dot(maps_ref[80:96, :], cotangent_ref[...], NT)).astype(jnp.bfloat16)
    sums[...] = jnp.zeros_like(sums)

    limit = end_ref[0, 0] * BLOCK_TOKENS

    def one_head(head, carry):
        piece = head // PIECE_HEADS
        inner = lax.rem(head, PIECE_HEADS)

        @pl.when(inner == 0)
        def _():
            own_copy(piece).wait()
            for slot in range(chips):
                across(piece, slot).wait_recv()

        columns = pl.ds(pl.multiple_of(head * GROUP_WIDTH, GROUP_WIDTH), GROUP_WIDTH)
        key_columns = pl.ds(pl.multiple_of(head * HEAD_DIM, HEAD_DIM), HEAD_DIM)
        value_columns = pl.ds(pl.multiple_of((KV_HEADS + head) * HEAD_DIM, HEAD_DIM), HEAD_DIM)
        down_out = maps_ref[48:64, columns]
        up_query = maps_ref[64:80, columns]
        up_pair = jnp.concatenate([pairs_ref[head * lanes + i] for i in range(lanes)], axis=1)

        queries = (
            query_ref[:, columns].astype(jnp.float32) + adapter_scale * dot(low_t[:, 0:16], up_query)
        ).astype(jnp.bfloat16)
        own_key = (
            own_ref[:, key_columns].astype(jnp.float32) + adapter_scale * dot(low_t[:, 16:32], up_pair[0:16])
        ).astype(jnp.bfloat16)
        own_value = (
            own_ref[:, value_columns].astype(jnp.float32) + adapter_scale * dot(low_t[:, 32:48], up_pair[16:32])
        ).astype(jnp.bfloat16)
        context_grad = (
            context_cotangent_ref[:, columns].astype(jnp.float32) + dot(up_out_t[...], down_out)
        ).astype(jnp.bfloat16)
        keys = rows_ref[piece, :, pl.ds(pl.multiple_of(inner * HEAD_DIM, HEAD_DIM), HEAD_DIM)]
        values = rows_ref[piece, :, pl.ds(pl.multiple_of(PIECE_WIDTH + inner * HEAD_DIM, HEAD_DIM), HEAD_DIM)]

        prompt_bias = jnp.where(
            lax.broadcasted_iota(jnp.int32, (1, prompt_len), 1) < limit, 0.0, masked_score
        )
        together = 2
        row = lax.broadcasted_iota(jnp.int32, (together * BLOCK_TOKENS, BLOCK_TOKENS), 0) % BLOCK_TOKENS
        column = lax.broadcasted_iota(jnp.int32, (together * BLOCK_TOKENS, BLOCK_TOKENS), 1)
        own_bias = jnp.where(column <= row, 0.0, masked_score)

        def stack(array, first):
            return jnp.concatenate(
                [array[:, (first + i) * HEAD_DIM:(first + i + 1) * HEAD_DIM] for i in range(together)], axis=0
            )

        def side(array):
            return [array[i * BLOCK_TOKENS:(i + 1) * BLOCK_TOKENS] for i in range(together)]

        contexts, query_grads = [], []
        key_grad = jnp.zeros((BLOCK_TOKENS, HEAD_DIM), jnp.float32)
        value_grad = jnp.zeros((BLOCK_TOKENS, HEAD_DIM), jnp.float32)
        for first in range(0, HEAD_GROUP, together):
            q = stack(queries, first)
            g = stack(context_grad, first)
            scores = dot(q, keys, NT) + prompt_bias
            own_scores = dot(q, own_key, NT) + own_bias
            peak = jnp.maximum(
                jnp.max(scores, axis=1, keepdims=True), jnp.max(own_scores, axis=1, keepdims=True)
            )
            exponent = jnp.exp2((scores - peak) * (inverse_root * LOG2E))
            own_exponent = jnp.exp2((own_scores - peak) * (inverse_root * LOG2E))
            total = jnp.sum(exponent, axis=1, keepdims=True) + jnp.sum(own_exponent, axis=1, keepdims=True)
            share = 1.0 / total
            weighted = dot(exponent.astype(jnp.bfloat16), values) + dot(own_exponent.astype(jnp.bfloat16), own_value)
            context = (weighted * share).astype(jnp.bfloat16)
            delta = jnp.sum(g.astype(jnp.float32) * context.astype(jnp.float32), axis=1, keepdims=True)
            score_grad = (exponent * share * (dot(g, values, NT) - delta)).astype(jnp.bfloat16)
            own_attention = own_exponent * share
            own_score_grad = (own_attention * (dot(g, own_value, NT) - delta)).astype(jnp.bfloat16)
            query_grad = ((dot(score_grad, keys) + dot(own_score_grad, own_key)) * inverse_root).astype(jnp.bfloat16)
            key_grad += dot(own_score_grad, q, TN)
            value_grad += dot(own_attention.astype(jnp.bfloat16), g, TN)
            contexts += side(context)
            query_grads += side(query_grad)
        context = jnp.concatenate(contexts, axis=1)
        query_grad = jnp.concatenate(query_grads, axis=1)
        key_grad = (key_grad * inverse_root).astype(jnp.bfloat16)
        value_grad = value_grad.astype(jnp.bfloat16)

        sums[0:16, :] += dot(up_query, query_grad, NT)
        sums[16:32, :] += dot(up_pair[0:16], key_grad, NT)
        sums[32:48, :] += dot(up_pair[16:32], value_grad, NT)
        sums[48:64, :] += dot(down_out, context, NT)
        grads_ref[48:64, columns] = dot(up_out[...], context).astype(jnp.bfloat16)
        grads_ref[64:80, columns] = (adapter_scale * dot(low[0:16, :], query_grad)).astype(jnp.bfloat16)
        pair_grad = jnp.concatenate(
            [dot(low[16:32, :], key_grad), dot(low[32:48, :], value_grad)], axis=0
        ) * adapter_scale
        pair_grad = pair_grad.astype(jnp.bfloat16)
        for i in range(lanes):
            pair_grads_ref[head * lanes + i] = pair_grad[:, i * pair_columns:(i + 1) * pair_columns]


        following = piece + 1
        for turn in range(PIECE_HEADS):
            @pl.when((inner == turn) & (following < PIECES))
            def _():
                for step in range(1 + turn * half // PIECE_HEADS, 1 + (turn + 1) * half // PIECE_HEADS):
                    hop(following, step)

        @pl.when((inner == PIECE_HEADS - 1) & (following + 1 < PIECES))
        def _():
            begin(following + 1)

        return carry

    lax.fori_loop(0, KV_HEADS, one_head, 0)

    up_low = (adapter_scale * sums[0:48, :]).astype(jnp.bfloat16)
    out_low = sums[48:64, :].astype(jnp.bfloat16)
    grads_ref[0:48, :] = dot(up_low, x_ref[...]).astype(jnp.bfloat16)
    grads_ref[80:96, :] = (adapter_scale * dot(out_low, cotangent_ref[...])).astype(jnp.bfloat16)

    for copy in parts:
        copy.wait_send()
    for piece in range(PIECES):
        for step in range(1, half + 1):
            for direction in range(2):
                ring(piece, direction, step).wait_send()
        for slot in range(chips):
            across(piece, slot).wait_send()


def block_gradients(n, end, x, query, own_pair, cotangent, context_cotangent, send_down, send_up, send_pair, prompt):
    tokens, width = x.shape
    map_rows = send_down.shape[1] + send_up.shape[1]
    chips = n // 2
    steps = chips // 2 + 1
    any_spec = pl.BlockSpec(memory_space=pl.ANY)
    vmem = pl.BlockSpec(memory_space=pltpu.VMEM)
    return pl.pallas_call(
        functools.partial(block_kernel, n),
        out_shape=(
            jax.ShapeDtypeStruct((map_rows, width), jnp.bfloat16),
            jax.ShapeDtypeStruct(send_pair.shape, jnp.bfloat16),
        ),
        in_specs=[pl.BlockSpec(memory_space=pltpu.SMEM)] + [vmem] * 5 + [any_spec] * 4,
        out_specs=(vmem, vmem),
        scratch_shapes=[
            pltpu.VMEM((map_rows, width), jnp.bfloat16),
            pltpu.VMEM(send_pair.shape, jnp.bfloat16),
            pltpu.VMEM((PIECES, n * prompt.shape[1], prompt.shape[2]), jnp.bfloat16),
            pltpu.VMEM((tokens, 48), jnp.bfloat16),
            pltpu.VMEM((48, tokens), jnp.bfloat16),
            pltpu.VMEM((16, tokens), jnp.bfloat16),
            pltpu.VMEM((tokens, 16), jnp.bfloat16),
            pltpu.VMEM((64, tokens), jnp.float32),
            pltpu.SemaphoreType.DMA((3,)),
            pltpu.SemaphoreType.DMA((PIECES,)),
            pltpu.SemaphoreType.DMA((PIECES, 2, steps)),
            pltpu.SemaphoreType.DMA((PIECES, 2, steps)),
            pltpu.SemaphoreType.DMA((PIECES, chips)),
            pltpu.SemaphoreType.DMA((PIECES, chips)),
            pltpu.SemaphoreType.DMA((3, n)),
            pltpu.SemaphoreType.DMA((3, n)),
        ],
        compiler_params=pltpu.CompilerParams(
            collective_id=0, has_side_effects=True, vmem_limit_bytes=48 * 1024 * 1024
        ),
    )(end, x, query, own_pair, cotangent, context_cotangent, send_down, send_up, send_pair, prompt)


def total_kernel(groups, n, ids_ref, back_ref, back_pair_ref, down_ref, up_ref, pair_ref):
    down_ref[...] = jnp.zeros_like(down_ref)
    up_ref[...] = jnp.zeros_like(up_ref)
    pair_ref[...] = jnp.zeros_like(pair_ref)
    for group in range(groups):
        def step(source, carry):
            adapter = ids_ref[group, 0, source]
            for part in range(4):
                down_ref[adapter, part] += back_ref[group, source, 16 * part:16 * (part + 1)].astype(jnp.float32)
            for part in range(2):
                up_ref[adapter, part] += back_ref[group, source, 64 + 16 * part:80 + 16 * part].astype(jnp.float32)
                pair_ref[adapter, part] += back_pair_ref[group, source, 16 * part:16 * (part + 1)].astype(jnp.float32)
            return carry

        lax.fori_loop(0, n, step, 0)


def totals(ids, back, back_pair):
    groups, n, _, columns = back.shape
    vmem = pl.BlockSpec(memory_space=pltpu.VMEM)
    return pl.pallas_call(
        functools.partial(total_kernel, groups, n),
        out_shape=(
            jax.ShapeDtypeStruct((ADAPTER_COUNT, 4, RANK, columns), jnp.float32),
            jax.ShapeDtypeStruct((ADAPTER_COUNT, 2, RANK, columns), jnp.float32),
            jax.ShapeDtypeStruct((ADAPTER_COUNT, 2, RANK, back_pair.shape[3]), jnp.float32),
        ),
        in_specs=[pl.BlockSpec(memory_space=pltpu.SMEM), vmem, vmem],
        out_specs=(vmem, vmem, vmem),
        compiler_params=pltpu.CompilerParams(vmem_limit_bytes=48 * 1024 * 1024),
    )(ids, back, back_pair)


def body(
    groups, n,
    candidate_hidden,
    frozen_query,
    candidate_key_value,
    prompt_key_value,
    candidate_adapter,
    prompt_block_end,
    adapter_down,
    adapter_up,
    adapter_up_key_value,
    output_cotangent,
    context_cotangent,
):
    ids = candidate_adapter[0]
    columns = adapter_down.shape[3]
    send_down = adapter_down[ids].reshape(n, 4 * RANK, columns)
    send_up = adapter_up[ids].reshape(n, 2 * RANK, columns)
    send_pair = adapter_up_key_value[ids].reshape(n, 2 * RANK, adapter_up_key_value.shape[3])
    rows = prompt_key_value.shape[1]
    prompt = jnp.transpose(
        prompt_key_value[0].reshape(rows, 2, PIECES, PIECE_WIDTH), (2, 0, 1, 3)
    ).reshape(PIECES, rows, 2 * PIECE_WIDTH)
    grads, pair_grads = block_gradients(
        n, prompt_block_end, candidate_hidden[0], frozen_query[0], candidate_key_value[0],
        output_cotangent[0], context_cotangent[0], send_down, send_up, send_pair, prompt,
    )
    back, back_pair, all_ids = spread(groups, n, grads, pair_grads, candidate_adapter)
    return totals(all_ids, back, back_pair)


def solution(mesh):
    placed = (
        P("prompt", "wide", None),
        P("prompt", "wide", None),
        P("prompt", "wide", None),
        P("prompt", "wide", None),
        P("prompt", None),
        P("prompt", "wide"),
        P(None, None, None, "wide"),
        P(None, None, None, "wide"),
        P(None, None, None, "wide"),
        P("prompt", "wide", None),
        P("prompt", "wide", None),
    )
    return jax.shard_map(
        functools.partial(body, mesh.shape["prompt"], mesh.shape["wide"]),
        mesh=mesh,
        in_specs=placed,
        out_specs=(
            P(None, None, None, "wide"),
            P(None, None, None, "wide"),
            P(None, None, None, "wide"),
        ),
        check_vma=False,
    )
```

```python
import functools

import jax
import jax.numpy as jnp
from jax import lax
from jax.experimental import pallas as pl
from jax.experimental.pallas import tpu as pltpu
from jax.sharding import PartitionSpec as P

HEADS = 32
KV_HEADS = 8
HEAD_DIM = 128
ADAPTER_COUNT = 16
BLOCK_TOKENS = 128
RANK = 16
HEAD_GROUP = HEADS // KV_HEADS
GROUP_WIDTH = HEAD_GROUP * HEAD_DIM
MESH = pl.DeviceIdType.MESH

adapter_scale = 2.0
masked_score = -1e30
LOG2E = 1.4426950408889634


def dot(a, b, contract=((1,), (0,))):
    return lax.dot_general(a, b, (contract, ((), ())), preferred_element_type=jnp.float32)


NT = ((1,), (1,))
TN = ((0,), (0,))


def chip_at(place, chips):
    place = lax.rem(place + chips, chips)
    return jnp.where(place < chips // 2, 2 * place, 2 * (chips - 1 - place) + 1)


PIECES = 2
PIECE_HEADS = KV_HEADS // PIECES
PIECE_WIDTH = PIECE_HEADS * HEAD_DIM


def block_kernel(groups, n, end_ref, x_in, query_in, own_in, cotangent_in, context_cotangent_in,
                 send_down_ref, send_up_ref, send_pair_ref, prompt_ref, ids_ref,
                 back_ref, back_pair_ref, all_ids_ref,
                 x_ref, query_ref, own_ref, cotangent_ref, context_cotangent_ref,
                 grads_ref, pair_grads_ref,
                 maps_ref, pairs_ref, rows_ref, low_t, low, up_out, up_out_t, sums,
                 local_sem, own_sem, ring_send, ring_recv, core_send, core_recv, part_send, part_recv,
                 load_sem, stay_sem, ids_send, ids_recv, early_send, early_recv, early_far_send, early_far_recv,
                 late_send, late_recv, late_far_send, late_far_recv):
    p = lax.axis_index("prompt")
    w = lax.axis_index("wide")
    chips = n // 2
    half = chips // 2
    core = lax.rem(w, 2)
    chip = w // 2
    place = jnp.where(lax.rem(chip, 2) == 0, chip // 2, chips - 1 - chip // 2)
    rows = prompt_ref.shape[1]
    cut = rows // 2
    map_columns = send_down_ref.shape[2]
    partner = w + 1 - 2 * core
    ahead = 2 * chip_at(place + 1, chips) + core
    behind = 2 * chip_at(place - 1, chips) + core

    barrier = pltpu.get_barrier_semaphore()
    for k in range(1, n):
        pl.semaphore_signal(barrier, inc=1, device_id=(p, lax.rem(w + k, n)), device_id_type=MESH)
    for k in range(1, groups):
        pl.semaphore_signal(barrier, inc=1, device_id=(lax.rem(p + k, groups), w), device_id_type=MESH)
    loads = [
        pltpu.make_async_copy(src, dst, load_sem.at[i])
        for i, (src, dst) in enumerate((
            (x_in, x_ref), (cotangent_in, cotangent_ref), (query_in, query_ref), (own_in, own_ref),
            (context_cotangent_in, context_cotangent_ref),
        ))
    ]
    for copy in loads:
        copy.start()
    pl.semaphore_wait(barrier, n + groups - 2)

    def shard(offset):
        return 2 * chip_at(place + offset, chips) + core

    def remote(src, dst, send, recv, to):
        return pltpu.make_async_remote_copy(
            src_ref=src, dst_ref=dst, send_sem=send, recv_sem=recv, device_id=(p, to), device_id_type=MESH
        )

    def window(piece, owner, start, size):
        return rows_ref.at[piece, pl.ds(pl.multiple_of(owner * rows + start, 16), size), :]

    def ring(piece, direction, step):
        owner = shard(1 - step) if direction == 0 else shard(step - 1)
        if step < half:
            start, size = 0, rows
        else:
            start, size = (0, cut) if direction == 0 else (cut, rows - cut)
        if step == 1:
            src = prompt_ref.at[piece, pl.ds(start, size), :]
        else:
            src = window(piece, owner, start, size)
        return remote(
            src, window(piece, owner, start, size), ring_send.at[piece, direction, step],
            ring_recv.at[piece, direction, step], ahead if direction == 0 else behind,
        )

    def across(piece, slot):
        if slot == 0:
            src, owner = prompt_ref.at[piece], w
        else:
            step = (slot + 1) // 2
            owner = shard(-step) if slot % 2 == 1 else shard(step)
            src = window(piece, owner, 0, rows)
        return remote(
            src, window(piece, owner, 0, rows), core_send.at[piece, slot], core_recv.at[piece, slot], partner
        )

    def own_copy(piece):
        return pltpu.make_async_copy(prompt_ref.at[piece], window(piece, w, 0, rows), own_sem.at[piece])

    def begin(piece):
        ring(piece, 0, 1).start()
        ring(piece, 1, 1).start()
        across(piece, 0).start()
        own_copy(piece).start()

    def hop(piece, step):
        for direction in range(2):
            ring(piece, direction, step).wait_recv()
            if step < half:
                ring(piece, direction, step + 1).start()
        across(piece, 2 * step - 1).start()
        if step < half:
            across(piece, 2 * step).start()

    def send_far(k, src, dst, send, recv):
        return pltpu.make_async_remote_copy(
            src_ref=src, dst_ref=dst, send_sem=send, recv_sem=recv,
            device_id=(lax.rem(p + k, groups), w), device_id_type=MESH,
        )

    owners = n // KV_HEADS
    first_head = w // owners

    def columns_of(owner):
        return pl.ds(pl.multiple_of(owner * map_columns, 128), map_columns)

    def early(owner):
        return (
            remote(grads_ref.at[64:96, columns_of(owner)], back_ref.at[p, w, 64:96],
                   early_send.at[0, owner], early_recv.at[0, w], owner),
            remote(pair_grads_ref.at[owner], back_pair_ref.at[p, w],
                   early_send.at[1, owner], early_recv.at[1, w], owner),
        )

    def early_from(source):
        return (
            remote(grads_ref.at[64:96, columns_of(w)], back_ref.at[p, source, 64:96],
                   early_send.at[0, source], early_recv.at[0, source], source),
            remote(pair_grads_ref.at[w], back_pair_ref.at[p, source],
                   early_send.at[1, source], early_recv.at[1, source], source),
        )

    def early_far(k, source, own):
        src = grads_ref.at[64:96, columns_of(w)] if own else back_ref.at[p, source, 64:96]
        src_pair = pair_grads_ref.at[w] if own else back_pair_ref.at[p, source]
        return (
            send_far(k, src, back_ref.at[p, source, 64:96],
                     early_far_send.at[0, k, source], early_far_recv.at[0, k, source]),
            send_far(k, src_pair, back_pair_ref.at[p, source],
                     early_far_send.at[1, k, source], early_far_recv.at[1, k, source]),
        )

    def stay_early():
        return (
            pltpu.make_async_copy(grads_ref.at[64:96, columns_of(w)], back_ref.at[p, w, 64:96], stay_sem.at[0]),
            pltpu.make_async_copy(pair_grads_ref.at[w], back_pair_ref.at[p, w], stay_sem.at[1]),
        )

    def forward_early():
        def one(offset, carry):
            source = lax.rem(w + offset, n)
            for copy in early_from(source):
                copy.wait_recv()
            for k in range(1, groups):
                for copy in early_far(k, source, False):
                    copy.start()
            return carry

        lax.fori_loop(1, n, one, 0)

    id_copies = [
        send_far(k, ids_ref, all_ids_ref.at[p], ids_send.at[k], ids_recv.at[k]) for k in range(1, groups)
    ]
    id_copies.append(pltpu.make_async_copy(ids_ref, all_ids_ref.at[p], stay_sem.at[3]))
    for copy in id_copies:
        copy.start()

    part_columns = pl.ds(pl.multiple_of(w * map_columns, 128), map_columns)
    down_here = maps_ref.at[0:64, part_columns]
    up_here = maps_ref.at[64:96, part_columns]
    pair_here = pairs_ref.at[w]
    locals_ = [
        pltpu.make_async_copy(send_down_ref.at[w], down_here, local_sem.at[0]),
        pltpu.make_async_copy(send_up_ref.at[w], up_here, local_sem.at[1]),
        pltpu.make_async_copy(send_pair_ref.at[w], pair_here, local_sem.at[2]),
    ]
    for copy in locals_:
        copy.start()
    parts = []
    for k in range(1, n):
        to = lax.rem(w + k, n)
        for i, (src, dst) in enumerate((
            (send_down_ref.at[to], down_here), (send_up_ref.at[to], up_here), (send_pair_ref.at[to], pair_here)
        )):
            copy = remote(src, dst, part_send.at[i, k], part_recv.at[i, k], to)
            copy.start()
            parts.append(copy)
    begin(0)
    for step in range(1, half + 1):
        hop(0, step)
    begin(1)
    for copy in locals_:
        copy.wait()
    for copy in parts:
        copy.wait_recv()

    for copy in loads:
        copy.wait()

    inverse_root = HEAD_DIM ** (-0.5)
    pair_columns = pairs_ref.shape[2]
    lanes = HEAD_DIM // pair_columns
    prompt_len = rows_ref.shape[1]

    x = x_ref[...]
    low_t[...] = dot(x, maps_ref[0:48, :], NT).astype(jnp.bfloat16)
    low[...] = dot(maps_ref[0:48, :], x, NT).astype(jnp.bfloat16)
    up_out_t[...] = (adapter_scale * dot(cotangent_ref[...], maps_ref[80:96, :], NT)).astype(jnp.bfloat16)
    up_out[...] = (adapter_scale * dot(maps_ref[80:96, :], cotangent_ref[...], NT)).astype(jnp.bfloat16)
    sums[...] = jnp.zeros_like(sums)

    limit = end_ref[0, 0] * BLOCK_TOKENS

    def one_head(head, carry):
        piece = head // PIECE_HEADS
        inner = lax.rem(head, PIECE_HEADS)

        @pl.when(inner == 0)
        def _():
            own_copy(piece).wait()
            for slot in range(chips):
                across(piece, slot).wait_recv()

        columns = pl.ds(pl.multiple_of(head * GROUP_WIDTH, GROUP_WIDTH), GROUP_WIDTH)
        key_columns = pl.ds(pl.multiple_of(head * HEAD_DIM, HEAD_DIM), HEAD_DIM)
        value_columns = pl.ds(pl.multiple_of((KV_HEADS + head) * HEAD_DIM, HEAD_DIM), HEAD_DIM)
        down_out = maps_ref[48:64, columns]
        up_query = maps_ref[64:80, columns]
        up_pair = jnp.concatenate([pairs_ref[head * lanes + i] for i in range(lanes)], axis=1)

        queries = (
            query_ref[:, columns].astype(jnp.float32) + adapter_scale * dot(low_t[:, 0:16], up_query)
        ).astype(jnp.bfloat16)
        own_key = (
            own_ref[:, key_columns].astype(jnp.float32) + adapter_scale * dot(low_t[:, 16:32], up_pair[0:16])
        ).astype(jnp.bfloat16)
        own_value = (
            own_ref[:, value_columns].astype(jnp.float32) + adapter_scale * dot(low_t[:, 32:48], up_pair[16:32])
        ).astype(jnp.bfloat16)
        context_grad = (
            context_cotangent_ref[:, columns].astype(jnp.float32) + dot(up_out_t[...], down_out)
        ).astype(jnp.bfloat16)
        keys = rows_ref[piece, :, pl.ds(pl.multiple_of(inner * HEAD_DIM, HEAD_DIM), HEAD_DIM)]
        values = rows_ref[piece, :, pl.ds(pl.multiple_of(PIECE_WIDTH + inner * HEAD_DIM, HEAD_DIM), HEAD_DIM)]

        prompt_bias = jnp.where(
            lax.broadcasted_iota(jnp.int32, (1, prompt_len), 1) < limit, 0.0, masked_score
        )
        together = 2
        row = lax.broadcasted_iota(jnp.int32, (together * BLOCK_TOKENS, BLOCK_TOKENS), 0) % BLOCK_TOKENS
        column = lax.broadcasted_iota(jnp.int32, (together * BLOCK_TOKENS, BLOCK_TOKENS), 1)
        own_bias = jnp.where(column <= row, 0.0, masked_score)

        def stack(array, first):
            return jnp.concatenate(
                [array[:, (first + i) * HEAD_DIM:(first + i + 1) * HEAD_DIM] for i in range(together)], axis=0
            )

        def side(array):
            return [array[i * BLOCK_TOKENS:(i + 1) * BLOCK_TOKENS] for i in range(together)]

        contexts, query_grads = [], []
        key_grad = jnp.zeros((BLOCK_TOKENS, HEAD_DIM), jnp.float32)
        value_grad = jnp.zeros((BLOCK_TOKENS, HEAD_DIM), jnp.float32)
        for first in range(0, HEAD_GROUP, together):
            q = stack(queries, first)
            g = stack(context_grad, first)
            scores = dot(q, keys, NT) + prompt_bias
            own_scores = dot(q, own_key, NT) + own_bias
            peak = jnp.maximum(
                jnp.max(scores, axis=1, keepdims=True), jnp.max(own_scores, axis=1, keepdims=True)
            )
            exponent = jnp.exp2((scores - peak) * (inverse_root * LOG2E))
            own_exponent = jnp.exp2((own_scores - peak) * (inverse_root * LOG2E))
            total = jnp.sum(exponent, axis=1, keepdims=True) + jnp.sum(own_exponent, axis=1, keepdims=True)
            share = 1.0 / total
            weighted = dot(exponent.astype(jnp.bfloat16), values) + dot(own_exponent.astype(jnp.bfloat16), own_value)
            context = (weighted * share).astype(jnp.bfloat16)
            delta = jnp.sum(g.astype(jnp.float32) * context.astype(jnp.float32), axis=1, keepdims=True)
            score_grad = (exponent * share * (dot(g, values, NT) - delta)).astype(jnp.bfloat16)
            own_attention = own_exponent * share
            own_score_grad = (own_attention * (dot(g, own_value, NT) - delta)).astype(jnp.bfloat16)
            query_grad = ((dot(score_grad, keys) + dot(own_score_grad, own_key)) * inverse_root).astype(jnp.bfloat16)
            key_grad += dot(own_score_grad, q, TN)
            value_grad += dot(own_attention.astype(jnp.bfloat16), g, TN)
            contexts += side(context)
            query_grads += side(query_grad)
        context = jnp.concatenate(contexts, axis=1)
        query_grad = jnp.concatenate(query_grads, axis=1)
        key_grad = (key_grad * inverse_root).astype(jnp.bfloat16)
        value_grad = value_grad.astype(jnp.bfloat16)

        sums[0:16, :] += dot(up_query, query_grad, NT)
        sums[16:32, :] += dot(up_pair[0:16], key_grad, NT)
        sums[32:48, :] += dot(up_pair[16:32], value_grad, NT)
        sums[48:64, :] += dot(down_out, context, NT)
        grads_ref[64:80, columns] = dot(up_out[...], context).astype(jnp.bfloat16)
        grads_ref[80:96, columns] = (adapter_scale * dot(low[0:16, :], query_grad)).astype(jnp.bfloat16)
        pair_grad = jnp.concatenate(
            [dot(low[16:32, :], key_grad), dot(low[32:48, :], value_grad)], axis=0
        ) * adapter_scale
        pair_grad = pair_grad.astype(jnp.bfloat16)
        for i in range(lanes):
            pair_grads_ref[head * lanes + i] = pair_grad[:, i * pair_columns:(i + 1) * pair_columns]


        for i in range(owners):
            owner = head * owners + i

            @pl.when(owner != w)
            def _():
                for copy in early(owner):
                    copy.start()

            @pl.when(owner == w)
            def _():
                for copy in stay_early():
                    copy.start()
                for k in range(1, groups):
                    for copy in early_far(k, w, True):
                        copy.start()

        @pl.when(head == first_head + 1)
        def _():
            forward_early()

        following = piece + 1
        for turn in range(PIECE_HEADS):
            @pl.when((inner == turn) & (following < PIECES))
            def _():
                for step in range(1 + turn * half // PIECE_HEADS, 1 + (turn + 1) * half // PIECE_HEADS):
                    hop(following, step)

        @pl.when((inner == PIECE_HEADS - 1) & (following + 1 < PIECES))
        def _():
            begin(following + 1)

        return carry

    lax.fori_loop(0, KV_HEADS, one_head, 0)

    up_low = (adapter_scale * sums[0:48, :]).astype(jnp.bfloat16)
    out_low = sums[48:64, :].astype(jnp.bfloat16)
    grads_ref[0:48, :] = dot(up_low, x_ref[...]).astype(jnp.bfloat16)
    grads_ref[48:64, :] = (adapter_scale * dot(out_low, cotangent_ref[...])).astype(jnp.bfloat16)

    late = []
    for k in range(1, n):
        to = lax.rem(w + k, n)
        copy = remote(
            grads_ref.at[0:64, columns_of(to)], back_ref.at[p, w, 0:64], late_send.at[k], late_recv.at[k], to
        )
        copy.start()
        late.append(copy)
    stay = pltpu.make_async_copy(grads_ref.at[0:64, columns_of(w)], back_ref.at[p, w, 0:64], stay_sem.at[2])
    stay.start()
    far = [
        send_far(k, grads_ref.at[0:64, columns_of(w)], back_ref.at[p, w, 0:64],
                 late_far_send.at[k, 0], late_far_recv.at[k, 0])
        for k in range(1, groups)
    ]
    for copy in far:
        copy.start()

    @pl.when(first_head == KV_HEADS - 1)
    def _():
        forward_early()

    for j in range(1, n):
        source = lax.rem(w - j + n, n)
        late[j - 1].wait_recv()
        for k in range(1, groups):
            here = back_ref.at[p, source, 0:64]
            copy = send_far(k, here, here, late_far_send.at[k, j], late_far_recv.at[k, j])
            copy.start()
            far.append(copy)

    for copy in late + parts:
        copy.wait_send()
    for copy in stay_early():
        copy.wait()
    stay.wait()

    def finish(offset, carry):
        other = lax.rem(w + offset, n)
        for copy in early(other):
            copy.wait_send()
        for k in range(1, groups):
            for copy in early_far(k, other, False):
                copy.wait_send()
                copy.wait_recv()
        return carry

    lax.fori_loop(1, n, finish, 0)
    for k in range(1, groups):
        for copy in early_far(k, w, True):
            copy.wait_send()
            copy.wait_recv()
    for copy in far + id_copies[:-1]:
        copy.wait_send()
        copy.wait_recv()
    id_copies[-1].wait()
    for piece in range(PIECES):
        for step in range(1, half + 1):
            for direction in range(2):
                ring(piece, direction, step).wait_send()
        for slot in range(chips):
            across(piece, slot).wait_send()


def block_gradients(groups, n, end, x, query, own_pair, cotangent, context_cotangent, send_down, send_up, send_pair,
                    prompt, ids):
    tokens, width = x.shape
    map_rows = send_down.shape[1] + send_up.shape[1]
    chips = n // 2
    steps = chips // 2 + 1
    any_spec = pl.BlockSpec(memory_space=pl.ANY)
    return pl.pallas_call(
        functools.partial(block_kernel, groups, n),
        out_shape=(
            jax.ShapeDtypeStruct((groups, n, map_rows, width // n), jnp.bfloat16),
            jax.ShapeDtypeStruct((groups,) + send_pair.shape, jnp.bfloat16),
            jax.ShapeDtypeStruct((groups,) + ids.shape, jnp.int32),
        ),
        in_specs=[pl.BlockSpec(memory_space=pltpu.SMEM)] + [any_spec] * 10,
        out_specs=(any_spec,) * 3,
        scratch_shapes=[
            pltpu.VMEM(x.shape, jnp.bfloat16),
            pltpu.VMEM(query.shape, jnp.bfloat16),
            pltpu.VMEM(own_pair.shape, jnp.bfloat16),
            pltpu.VMEM(cotangent.shape, jnp.bfloat16),
            pltpu.VMEM(context_cotangent.shape, jnp.bfloat16),
            pltpu.VMEM((map_rows, width), jnp.bfloat16),
            pltpu.VMEM(send_pair.shape, jnp.bfloat16),
            pltpu.VMEM((map_rows, width), jnp.bfloat16),
            pltpu.VMEM(send_pair.shape, jnp.bfloat16),
            pltpu.VMEM((PIECES, n * prompt.shape[1], prompt.shape[2]), jnp.bfloat16),
            pltpu.VMEM((tokens, 48), jnp.bfloat16),
            pltpu.VMEM((48, tokens), jnp.bfloat16),
            pltpu.VMEM((16, tokens), jnp.bfloat16),
            pltpu.VMEM((tokens, 16), jnp.bfloat16),
            pltpu.VMEM((64, tokens), jnp.float32),
            pltpu.SemaphoreType.DMA((3,)),
            pltpu.SemaphoreType.DMA((PIECES,)),
            pltpu.SemaphoreType.DMA((PIECES, 2, steps)),
            pltpu.SemaphoreType.DMA((PIECES, 2, steps)),
            pltpu.SemaphoreType.DMA((PIECES, chips)),
            pltpu.SemaphoreType.DMA((PIECES, chips)),
            pltpu.SemaphoreType.DMA((3, n)),
            pltpu.SemaphoreType.DMA((3, n)),
            pltpu.SemaphoreType.DMA((5,)),
            pltpu.SemaphoreType.DMA((4,)),
            pltpu.SemaphoreType.DMA((groups,)),
            pltpu.SemaphoreType.DMA((groups,)),
            pltpu.SemaphoreType.DMA((2, n)),
            pltpu.SemaphoreType.DMA((2, n)),
            pltpu.SemaphoreType.DMA((2, groups, n)),
            pltpu.SemaphoreType.DMA((2, groups, n)),
            pltpu.SemaphoreType.DMA((n,)),
            pltpu.SemaphoreType.DMA((n,)),
            pltpu.SemaphoreType.DMA((groups, n)),
            pltpu.SemaphoreType.DMA((groups, n)),
        ],
        compiler_params=pltpu.CompilerParams(
            collective_id=0, has_side_effects=True, vmem_limit_bytes=48 * 1024 * 1024
        ),
    )(end, x, query, own_pair, cotangent, context_cotangent, send_down, send_up, send_pair, prompt,
      ids)


def total_kernel(groups, n, ids_ref, back_ref, back_pair_ref, down_ref, up_ref, pair_ref):
    down_ref[...] = jnp.zeros_like(down_ref)
    up_ref[...] = jnp.zeros_like(up_ref)
    pair_ref[...] = jnp.zeros_like(pair_ref)
    for group in range(groups):
        def step(source, carry):
            adapter = ids_ref[group, 0, source]
            for part, start in enumerate((0, 16, 32, 64)):
                down_ref[adapter, part] += back_ref[group, source, start:start + 16].astype(jnp.float32)
            for part, start in enumerate((80, 48)):
                up_ref[adapter, part] += back_ref[group, source, start:start + 16].astype(jnp.float32)
            for part in range(2):
                pair_ref[adapter, part] += back_pair_ref[group, source, 16 * part:16 * (part + 1)].astype(jnp.float32)
            return carry

        lax.fori_loop(0, n, step, 0)


def totals(ids, back, back_pair):
    groups, n, _, columns = back.shape
    vmem = pl.BlockSpec(memory_space=pltpu.VMEM)
    return pl.pallas_call(
        functools.partial(total_kernel, groups, n),
        out_shape=(
            jax.ShapeDtypeStruct((ADAPTER_COUNT, 4, RANK, columns), jnp.float32),
            jax.ShapeDtypeStruct((ADAPTER_COUNT, 2, RANK, columns), jnp.float32),
            jax.ShapeDtypeStruct((ADAPTER_COUNT, 2, RANK, back_pair.shape[3]), jnp.float32),
        ),
        in_specs=[pl.BlockSpec(memory_space=pltpu.SMEM), vmem, vmem],
        out_specs=(vmem, vmem, vmem),
        compiler_params=pltpu.CompilerParams(vmem_limit_bytes=48 * 1024 * 1024),
    )(ids, back, back_pair)


def body(
    groups, n,
    candidate_hidden,
    frozen_query,
    candidate_key_value,
    prompt_key_value,
    candidate_adapter,
    prompt_block_end,
    adapter_down,
    adapter_up,
    adapter_up_key_value,
    output_cotangent,
    context_cotangent,
):
    ids = candidate_adapter[0]
    columns = adapter_down.shape[3]
    send_down = adapter_down[ids].reshape(n, 4 * RANK, columns)
    send_up = adapter_up[ids].reshape(n, 2 * RANK, columns)
    send_pair = adapter_up_key_value[ids].reshape(n, 2 * RANK, adapter_up_key_value.shape[3])
    rows = prompt_key_value.shape[1]
    prompt = jnp.transpose(
        prompt_key_value[0].reshape(rows, 2, PIECES, PIECE_WIDTH), (2, 0, 1, 3)
    ).reshape(PIECES, rows, 2 * PIECE_WIDTH)
    back, back_pair, all_ids = block_gradients(
        groups, n, prompt_block_end, candidate_hidden[0], frozen_query[0], candidate_key_value[0],
        output_cotangent[0], context_cotangent[0], send_down, send_up, send_pair, prompt,
        candidate_adapter,
    )
    return totals(all_ids, back, back_pair)


def solution(mesh):
    placed = (
        P("prompt", "wide", None),
        P("prompt", "wide", None),
        P("prompt", "wide", None),
        P("prompt", "wide", None),
        P("prompt", None),
        P("prompt", "wide"),
        P(None, None, None, "wide"),
        P(None, None, None, "wide"),
        P(None, None, None, "wide"),
        P("prompt", "wide", None),
        P("prompt", "wide", None),
    )
    return jax.shard_map(
        functools.partial(body, mesh.shape["prompt"], mesh.shape["wide"]),
        mesh=mesh,
        in_specs=placed,
        out_specs=(
            P(None, None, None, "wide"),
            P(None, None, None, "wide"),
            P(None, None, None, "wide"),
        ),
        check_vma=False,
    )
```

```python
import functools

import jax
import jax.numpy as jnp
from jax import lax
from jax.experimental import pallas as pl
from jax.experimental.pallas import tpu as pltpu
from jax.sharding import PartitionSpec as P

HEADS = 32
KV_HEADS = 8
HEAD_DIM = 128
ADAPTER_COUNT = 16
BLOCK_TOKENS = 128
RANK = 16
HEAD_GROUP = HEADS // KV_HEADS
GROUP_WIDTH = HEAD_GROUP * HEAD_DIM
MESH = pl.DeviceIdType.MESH

adapter_scale = 2.0
masked_score = -1e30
LOG2E = 1.4426950408889634


def dot(a, b, contract=((1,), (0,))):
    return lax.dot_general(a, b, (contract, ((), ())), preferred_element_type=jnp.float32)


NT = ((1,), (1,))
TN = ((0,), (0,))


def chip_at(place, chips):
    place = lax.rem(place + chips, chips)
    return jnp.where(place < chips // 2, 2 * place, 2 * (chips - 1 - place) + 1)


PIECES = 2
PIECE_HEADS = KV_HEADS // PIECES
PIECE_WIDTH = PIECE_HEADS * HEAD_DIM


def block_kernel(groups, n, end_ref, x_in, query_in, own_in, cotangent_in, context_cotangent_in,
                 send_down_ref, send_up_ref, send_pair_ref, prompt_ref, ids_ref,
                 back_ref, back_pair_ref, all_ids_ref,
                 x_ref, query_ref, own_ref, cotangent_ref, context_cotangent_ref,
                 grads_ref, pair_grads_ref,
                 maps_ref, pairs_ref, rows_ref, low_t, low, up_out, up_out_t, sums,
                 local_sem, own_sem, ring_send, ring_recv, core_send, core_recv, part_send, part_recv,
                 load_sem, stay_sem, ids_send, ids_recv, early_send, early_recv, early_far_send, early_far_recv,
                 late_send, late_recv, late_far_send, late_far_recv):
    p = lax.axis_index("prompt")
    w = lax.axis_index("wide")
    chips = n // 2
    half = chips // 2
    core = lax.rem(w, 2)
    chip = w // 2
    place = jnp.where(lax.rem(chip, 2) == 0, chip // 2, chips - 1 - chip // 2)
    rows = prompt_ref.shape[1]
    cut = rows // 2
    map_columns = send_down_ref.shape[2]
    partner = w + 1 - 2 * core
    ahead = 2 * chip_at(place + 1, chips) + core
    behind = 2 * chip_at(place - 1, chips) + core

    barrier = pltpu.get_barrier_semaphore()
    for k in range(1, n):
        pl.semaphore_signal(barrier, inc=1, device_id=(p, lax.rem(w + k, n)), device_id_type=MESH)
    for k in range(1, groups):
        pl.semaphore_signal(barrier, inc=1, device_id=(lax.rem(p + k, groups), w), device_id_type=MESH)
    loads = [
        pltpu.make_async_copy(src, dst, load_sem.at[i])
        for i, (src, dst) in enumerate((
            (x_in, x_ref), (cotangent_in, cotangent_ref), (query_in, query_ref), (own_in, own_ref),
            (context_cotangent_in, context_cotangent_ref),
        ))
    ]
    for copy in loads:
        copy.start()
    pl.semaphore_wait(barrier, n + groups - 2)

    def shard(offset):
        return 2 * chip_at(place + offset, chips) + core

    def remote(src, dst, send, recv, to):
        return pltpu.make_async_remote_copy(
            src_ref=src, dst_ref=dst, send_sem=send, recv_sem=recv, device_id=(p, to), device_id_type=MESH
        )

    def window(piece, owner, start, size):
        return rows_ref.at[piece, pl.ds(pl.multiple_of(owner * rows + start, 16), size), :]

    def ring(piece, direction, step):
        owner = shard(1 - step) if direction == 0 else shard(step - 1)
        if step < half:
            start, size = 0, rows
        else:
            start, size = (0, cut) if direction == 0 else (cut, rows - cut)
        if step == 1:
            src = prompt_ref.at[piece, pl.ds(start, size), :]
        else:
            src = window(piece, owner, start, size)
        return remote(
            src, window(piece, owner, start, size), ring_send.at[piece, direction, step],
            ring_recv.at[piece, direction, step], ahead if direction == 0 else behind,
        )

    def across(piece, slot):
        if slot == 0:
            src, owner = prompt_ref.at[piece], w
        else:
            step = (slot + 1) // 2
            owner = shard(-step) if slot % 2 == 1 else shard(step)
            src = window(piece, owner, 0, rows)
        return remote(
            src, window(piece, owner, 0, rows), core_send.at[piece, slot], core_recv.at[piece, slot], partner
        )

    def own_copy(piece):
        return pltpu.make_async_copy(prompt_ref.at[piece], window(piece, w, 0, rows), own_sem.at[piece])

    def begin(piece):
        ring(piece, 0, 1).start()
        ring(piece, 1, 1).start()
        across(piece, 0).start()
        own_copy(piece).start()

    def hop(piece, step):
        for direction in range(2):
            ring(piece, direction, step).wait_recv()
            if step < half:
                ring(piece, direction, step + 1).start()
        across(piece, 2 * step - 1).start()
        if step < half:
            across(piece, 2 * step).start()

    def send_far(k, src, dst, send, recv):
        return pltpu.make_async_remote_copy(
            src_ref=src, dst_ref=dst, send_sem=send, recv_sem=recv,
            device_id=(lax.rem(p + k, groups), w), device_id_type=MESH,
        )

    owners = n // KV_HEADS
    first_head = w // owners

    def columns_of(owner):
        return pl.ds(pl.multiple_of(owner * map_columns, 128), map_columns)

    def early(owner):
        return (
            remote(grads_ref.at[64:96, columns_of(owner)], back_ref.at[p, w, 64:96],
                   early_send.at[0, owner], early_recv.at[0, w], owner),
            remote(pair_grads_ref.at[owner], back_pair_ref.at[p, w],
                   early_send.at[1, owner], early_recv.at[1, w], owner),
        )

    def early_from(source):
        return (
            remote(grads_ref.at[64:96, columns_of(w)], back_ref.at[p, source, 64:96],
                   early_send.at[0, source], early_recv.at[0, source], source),
            remote(pair_grads_ref.at[w], back_pair_ref.at[p, source],
                   early_send.at[1, source], early_recv.at[1, source], source),
        )

    def early_far(k, source, own):
        src = grads_ref.at[64:96, columns_of(w)] if own else back_ref.at[p, source, 64:96]
        src_pair = pair_grads_ref.at[w] if own else back_pair_ref.at[p, source]
        return (
            send_far(k, src, back_ref.at[p, source, 64:96],
                     early_far_send.at[0, k, source], early_far_recv.at[0, k, source]),
            send_far(k, src_pair, back_pair_ref.at[p, source],
                     early_far_send.at[1, k, source], early_far_recv.at[1, k, source]),
        )

    def stay_early():
        return (
            pltpu.make_async_copy(grads_ref.at[64:96, columns_of(w)], back_ref.at[p, w, 64:96], stay_sem.at[0]),
            pltpu.make_async_copy(pair_grads_ref.at[w], back_pair_ref.at[p, w], stay_sem.at[1]),
        )

    def forward_early():
        def one(offset, carry):
            source = lax.rem(w + offset, n)
            for copy in early_from(source):
                copy.wait_recv()
            for k in range(1, groups):
                for copy in early_far(k, source, False):
                    copy.start()
            return carry

        lax.fori_loop(1, n, one, 0)

    id_copies = [
        send_far(k, ids_ref, all_ids_ref.at[p], ids_send.at[k], ids_recv.at[k]) for k in range(1, groups)
    ]
    id_copies.append(pltpu.make_async_copy(ids_ref, all_ids_ref.at[p], stay_sem.at[3]))
    for copy in id_copies:
        copy.start()

    part_columns = pl.ds(pl.multiple_of(w * map_columns, 128), map_columns)
    down_here = maps_ref.at[0:64, part_columns]
    up_here = maps_ref.at[64:96, part_columns]
    pair_here = pairs_ref.at[w]
    locals_ = [
        pltpu.make_async_copy(send_down_ref.at[w], down_here, local_sem.at[0]),
        pltpu.make_async_copy(send_up_ref.at[w], up_here, local_sem.at[1]),
        pltpu.make_async_copy(send_pair_ref.at[w], pair_here, local_sem.at[2]),
    ]
    for copy in locals_:
        copy.start()
    parts = []
    for k in range(1, n):
        to = lax.rem(w + k, n)
        for i, (src, dst) in enumerate((
            (send_down_ref.at[to], down_here), (send_up_ref.at[to], up_here), (send_pair_ref.at[to], pair_here)
        )):
            copy = remote(src, dst, part_send.at[i, k], part_recv.at[i, k], to)
            copy.start()
            parts.append(copy)
    begin(0)
    for step in range(1, half + 1):
        hop(0, step)
    begin(1)
    for copy in locals_:
        copy.wait()
    for copy in parts:
        copy.wait_recv()

    for copy in loads:
        copy.wait()

    inverse_root = HEAD_DIM ** (-0.5)
    pair_columns = pairs_ref.shape[2]
    lanes = HEAD_DIM // pair_columns
    prompt_len = rows_ref.shape[1]

    x = x_ref[...]
    low_t[...] = dot(x, maps_ref[0:48, :], NT).astype(jnp.bfloat16)
    low[...] = dot(maps_ref[0:48, :], x, NT).astype(jnp.bfloat16)
    up_out_t[...] = (adapter_scale * dot(cotangent_ref[...], maps_ref[80:96, :], NT)).astype(jnp.bfloat16)
    up_out[...] = (adapter_scale * dot(maps_ref[80:96, :], cotangent_ref[...], NT)).astype(jnp.bfloat16)
    sums[...] = jnp.zeros_like(sums)

    limit = end_ref[0, 0] * BLOCK_TOKENS

    def one_head(head, carry):
        piece = head // PIECE_HEADS
        inner = lax.rem(head, PIECE_HEADS)

        @pl.when(inner == 0)
        def _():
            own_copy(piece).wait()
            for slot in range(chips):
                across(piece, slot).wait_recv()

        columns = pl.ds(pl.multiple_of(head * GROUP_WIDTH, GROUP_WIDTH), GROUP_WIDTH)
        key_columns = pl.ds(pl.multiple_of(head * HEAD_DIM, HEAD_DIM), HEAD_DIM)
        value_columns = pl.ds(pl.multiple_of((KV_HEADS + head) * HEAD_DIM, HEAD_DIM), HEAD_DIM)
        down_out = maps_ref[48:64, columns]
        up_query = maps_ref[64:80, columns]
        up_pair = jnp.concatenate([pairs_ref[head * lanes + i] for i in range(lanes)], axis=1)

        queries = (
            query_ref[:, columns].astype(jnp.float32) + adapter_scale * dot(low_t[:, 0:16], up_query)
        ).astype(jnp.bfloat16)
        own_key = (
            own_ref[:, key_columns].astype(jnp.float32) + adapter_scale * dot(low_t[:, 16:32], up_pair[0:16])
        ).astype(jnp.bfloat16)
        own_value = (
            own_ref[:, value_columns].astype(jnp.float32) + adapter_scale * dot(low_t[:, 32:48], up_pair[16:32])
        ).astype(jnp.bfloat16)
        context_grad = (
            context_cotangent_ref[:, columns].astype(jnp.float32) + dot(up_out_t[...], down_out)
        ).astype(jnp.bfloat16)
        keys = rows_ref[piece, :, pl.ds(pl.multiple_of(inner * HEAD_DIM, HEAD_DIM), HEAD_DIM)]
        values = rows_ref[piece, :, pl.ds(pl.multiple_of(PIECE_WIDTH + inner * HEAD_DIM, HEAD_DIM), HEAD_DIM)]

        prompt_bias = jnp.where(
            lax.broadcasted_iota(jnp.int32, (1, prompt_len), 1) < limit, 0.0, masked_score
        )
        together = 2
        row = lax.broadcasted_iota(jnp.int32, (together * BLOCK_TOKENS, BLOCK_TOKENS), 0) % BLOCK_TOKENS
        column = lax.broadcasted_iota(jnp.int32, (together * BLOCK_TOKENS, BLOCK_TOKENS), 1)
        own_bias = jnp.where(column <= row, 0.0, masked_score)

        def stack(array, first):
            return jnp.concatenate(
                [array[:, (first + i) * HEAD_DIM:(first + i + 1) * HEAD_DIM] for i in range(together)], axis=0
            )

        def side(array):
            return [array[i * BLOCK_TOKENS:(i + 1) * BLOCK_TOKENS] for i in range(together)]

        contexts, query_grads = [], []
        key_grad = jnp.zeros((BLOCK_TOKENS, HEAD_DIM), jnp.float32)
        value_grad = jnp.zeros((BLOCK_TOKENS, HEAD_DIM), jnp.float32)
        for first in range(0, HEAD_GROUP, together):
            q = stack(queries, first)
            g = stack(context_grad, first)
            scores = dot(q, keys, NT) + prompt_bias
            own_scores = dot(q, own_key, NT) + own_bias
            peak = jnp.maximum(
                jnp.max(scores, axis=1, keepdims=True), jnp.max(own_scores, axis=1, keepdims=True)
            )
            exponent = jnp.exp2((scores - peak) * (inverse_root * LOG2E))
            own_exponent = jnp.exp2((own_scores - peak) * (inverse_root * LOG2E))
            total = jnp.sum(exponent, axis=1, keepdims=True) + jnp.sum(own_exponent, axis=1, keepdims=True)
            share = 1.0 / total
            weighted = dot(exponent.astype(jnp.bfloat16), values) + dot(own_exponent.astype(jnp.bfloat16), own_value)
            context = (weighted * share).astype(jnp.bfloat16)
            delta = jnp.sum(g.astype(jnp.float32) * context.astype(jnp.float32), axis=1, keepdims=True)
            score_grad = (exponent * share * (dot(g, values, NT) - delta)).astype(jnp.bfloat16)
            own_attention = own_exponent * share
            own_score_grad = (own_attention * (dot(g, own_value, NT) - delta)).astype(jnp.bfloat16)
            query_grad = ((dot(score_grad, keys) + dot(own_score_grad, own_key)) * inverse_root).astype(jnp.bfloat16)
            key_grad += dot(own_score_grad, q, TN)
            value_grad += dot(own_attention.astype(jnp.bfloat16), g, TN)
            contexts += side(context)
            query_grads += side(query_grad)
        context = jnp.concatenate(contexts, axis=1)
        query_grad = jnp.concatenate(query_grads, axis=1)
        key_grad = (key_grad * inverse_root).astype(jnp.bfloat16)
        value_grad = value_grad.astype(jnp.bfloat16)

        sums[0:16, :] += dot(up_query, query_grad, NT)
        sums[16:32, :] += dot(up_pair[0:16], key_grad, NT)
        sums[32:48, :] += dot(up_pair[16:32], value_grad, NT)
        sums[48:64, :] += dot(down_out, context, NT)
        grads_ref[64:80, columns] = dot(up_out[...], context).astype(jnp.bfloat16)
        grads_ref[80:96, columns] = (adapter_scale * dot(low[0:16, :], query_grad)).astype(jnp.bfloat16)
        pair_grad = jnp.concatenate(
            [dot(low[16:32, :], key_grad), dot(low[32:48, :], value_grad)], axis=0
        ) * adapter_scale
        pair_grad = pair_grad.astype(jnp.bfloat16)
        for i in range(lanes):
            pair_grads_ref[head * lanes + i] = pair_grad[:, i * pair_columns:(i + 1) * pair_columns]


        for i in range(owners):
            owner = head * owners + i

            @pl.when(owner != w)
            def _():
                for copy in early(owner):
                    copy.start()

            @pl.when(owner == w)
            def _():
                for copy in stay_early():
                    copy.start()
                for k in range(1, groups):
                    for copy in early_far(k, w, True):
                        copy.start()

        @pl.when(head == first_head + 1)
        def _():
            forward_early()

        following = piece + 1
        for turn in range(PIECE_HEADS):
            @pl.when((inner == turn) & (following < PIECES))
            def _():
                for step in range(1 + turn * half // PIECE_HEADS, 1 + (turn + 1) * half // PIECE_HEADS):
                    hop(following, step)

        @pl.when((inner == PIECE_HEADS - 1) & (following + 1 < PIECES))
        def _():
            begin(following + 1)

        return carry

    lax.fori_loop(0, KV_HEADS, one_head, 0)

    up_low = (adapter_scale * sums[0:48, :]).astype(jnp.bfloat16)
    out_low = sums[48:64, :].astype(jnp.bfloat16)
    grads_ref[0:48, :] = dot(up_low, x_ref[...]).astype(jnp.bfloat16)
    grads_ref[48:64, :] = (adapter_scale * dot(out_low, cotangent_ref[...])).astype(jnp.bfloat16)

    late = []
    for k in range(1, n):
        to = lax.rem(w + k, n)
        copy = remote(
            grads_ref.at[0:64, columns_of(to)], back_ref.at[p, w, 0:64], late_send.at[k], late_recv.at[k], to
        )
        copy.start()
        late.append(copy)
    stay = pltpu.make_async_copy(grads_ref.at[0:64, columns_of(w)], back_ref.at[p, w, 0:64], stay_sem.at[2])
    stay.start()
    far = [
        send_far(k, grads_ref.at[0:64, columns_of(w)], back_ref.at[p, w, 0:64],
                 late_far_send.at[k, 0], late_far_recv.at[k, 0])
        for k in range(1, groups)
    ]
    for copy in far:
        copy.start()

    @pl.when(first_head == KV_HEADS - 1)
    def _():
        forward_early()

    for j in range(1, n):
        source = lax.rem(w - j + n, n)
        late[j - 1].wait_recv()
        for k in range(1, groups):
            here = back_ref.at[p, source, 0:64]
            copy = send_far(k, here, here, late_far_send.at[k, j], late_far_recv.at[k, j])
            copy.start()
            far.append(copy)

    for copy in late + parts:
        copy.wait_send()
    for copy in stay_early():
        copy.wait()
    stay.wait()

    def finish(offset, carry):
        other = lax.rem(w + offset, n)
        for copy in early(other):
            copy.wait_send()
        for k in range(1, groups):
            for copy in early_far(k, other, False):
                copy.wait_send()
                copy.wait_recv()
        return carry

    lax.fori_loop(1, n, finish, 0)
    for k in range(1, groups):
        for copy in early_far(k, w, True):
            copy.wait_send()
            copy.wait_recv()
    for copy in far + id_copies[:-1]:
        copy.wait_send()
        copy.wait_recv()
    id_copies[-1].wait()
    for piece in range(PIECES):
        for step in range(1, half + 1):
            for direction in range(2):
                ring(piece, direction, step).wait_send()
        for slot in range(chips):
            across(piece, slot).wait_send()


def block_gradients(groups, n, end, x, query, own_pair, cotangent, context_cotangent, send_down, send_up, send_pair,
                    prompt, ids):
    tokens, width = x.shape
    map_rows = send_down.shape[1] + send_up.shape[1]
    chips = n // 2
    steps = chips // 2 + 1
    any_spec = pl.BlockSpec(memory_space=pl.ANY)
    return pl.pallas_call(
        functools.partial(block_kernel, groups, n),
        out_shape=(
            jax.ShapeDtypeStruct((groups, n, map_rows, width // n), jnp.bfloat16),
            jax.ShapeDtypeStruct((groups,) + send_pair.shape, jnp.bfloat16),
            jax.ShapeDtypeStruct((groups,) + ids.shape, jnp.int32),
        ),
        in_specs=[pl.BlockSpec(memory_space=pltpu.SMEM)] + [pl.BlockSpec(memory_space=pltpu.HBM)] * 5 + [any_spec] * 5,
        out_specs=(any_spec,) * 3,
        scratch_shapes=[
            pltpu.VMEM(x.shape, jnp.bfloat16),
            pltpu.VMEM(query.shape, jnp.bfloat16),
            pltpu.VMEM(own_pair.shape, jnp.bfloat16),
            pltpu.VMEM(cotangent.shape, jnp.bfloat16),
            pltpu.VMEM(context_cotangent.shape, jnp.bfloat16),
            pltpu.VMEM((map_rows, width), jnp.bfloat16),
            pltpu.VMEM(send_pair.shape, jnp.bfloat16),
            pltpu.VMEM((map_rows, width), jnp.bfloat16),
            pltpu.VMEM(send_pair.shape, jnp.bfloat16),
            pltpu.VMEM((PIECES, n * prompt.shape[1], prompt.shape[2]), jnp.bfloat16),
            pltpu.VMEM((tokens, 48), jnp.bfloat16),
            pltpu.VMEM((48, tokens), jnp.bfloat16),
            pltpu.VMEM((16, tokens), jnp.bfloat16),
            pltpu.VMEM((tokens, 16), jnp.bfloat16),
            pltpu.VMEM((64, tokens), jnp.float32),
            pltpu.SemaphoreType.DMA((3,)),
            pltpu.SemaphoreType.DMA((PIECES,)),
            pltpu.SemaphoreType.DMA((PIECES, 2, steps)),
            pltpu.SemaphoreType.DMA((PIECES, 2, steps)),
            pltpu.SemaphoreType.DMA((PIECES, chips)),
            pltpu.SemaphoreType.DMA((PIECES, chips)),
            pltpu.SemaphoreType.DMA((3, n)),
            pltpu.SemaphoreType.DMA((3, n)),
            pltpu.SemaphoreType.DMA((5,)),
            pltpu.SemaphoreType.DMA((4,)),
            pltpu.SemaphoreType.DMA((groups,)),
            pltpu.SemaphoreType.DMA((groups,)),
            pltpu.SemaphoreType.DMA((2, n)),
            pltpu.SemaphoreType.DMA((2, n)),
            pltpu.SemaphoreType.DMA((2, groups, n)),
            pltpu.SemaphoreType.DMA((2, groups, n)),
            pltpu.SemaphoreType.DMA((n,)),
            pltpu.SemaphoreType.DMA((n,)),
            pltpu.SemaphoreType.DMA((groups, n)),
            pltpu.SemaphoreType.DMA((groups, n)),
        ],
        compiler_params=pltpu.CompilerParams(
            collective_id=0, has_side_effects=True, vmem_limit_bytes=48 * 1024 * 1024
        ),
    )(end, x, query, own_pair, cotangent, context_cotangent, send_down, send_up, send_pair, prompt,
      ids)


def total_kernel(groups, n, ids_ref, back_ref, back_pair_ref, down_ref, up_ref, pair_ref):
    down_ref[...] = jnp.zeros_like(down_ref)
    up_ref[...] = jnp.zeros_like(up_ref)
    pair_ref[...] = jnp.zeros_like(pair_ref)
    for group in range(groups):
        def step(source, carry):
            adapter = ids_ref[group, 0, source]
            for part, start in enumerate((0, 16, 32, 64)):
                down_ref[adapter, part] += back_ref[group, source, start:start + 16].astype(jnp.float32)
            for part, start in enumerate((80, 48)):
                up_ref[adapter, part] += back_ref[group, source, start:start + 16].astype(jnp.float32)
            for part in range(2):
                pair_ref[adapter, part] += back_pair_ref[group, source, 16 * part:16 * (part + 1)].astype(jnp.float32)
            return carry

        lax.fori_loop(0, n, step, 0)


def totals(ids, back, back_pair):
    groups, n, _, columns = back.shape
    vmem = pl.BlockSpec(memory_space=pltpu.VMEM)
    return pl.pallas_call(
        functools.partial(total_kernel, groups, n),
        out_shape=(
            jax.ShapeDtypeStruct((ADAPTER_COUNT, 4, RANK, columns), jnp.float32),
            jax.ShapeDtypeStruct((ADAPTER_COUNT, 2, RANK, columns), jnp.float32),
            jax.ShapeDtypeStruct((ADAPTER_COUNT, 2, RANK, back_pair.shape[3]), jnp.float32),
        ),
        in_specs=[pl.BlockSpec(memory_space=pltpu.SMEM), vmem, vmem],
        out_specs=(vmem, vmem, vmem),
        compiler_params=pltpu.CompilerParams(vmem_limit_bytes=48 * 1024 * 1024),
    )(ids, back, back_pair)


def body(
    groups, n,
    candidate_hidden,
    frozen_query,
    candidate_key_value,
    prompt_key_value,
    candidate_adapter,
    prompt_block_end,
    adapter_down,
    adapter_up,
    adapter_up_key_value,
    output_cotangent,
    context_cotangent,
):
    ids = candidate_adapter[0]
    columns = adapter_down.shape[3]
    send_down = adapter_down[ids].reshape(n, 4 * RANK, columns)
    send_up = adapter_up[ids].reshape(n, 2 * RANK, columns)
    send_pair = adapter_up_key_value[ids].reshape(n, 2 * RANK, adapter_up_key_value.shape[3])
    rows = prompt_key_value.shape[1]
    prompt = jnp.transpose(
        prompt_key_value[0].reshape(rows, 2, PIECES, PIECE_WIDTH), (2, 0, 1, 3)
    ).reshape(PIECES, rows, 2 * PIECE_WIDTH)
    back, back_pair, all_ids = block_gradients(
        groups, n, prompt_block_end, candidate_hidden[0], frozen_query[0], candidate_key_value[0],
        output_cotangent[0], context_cotangent[0], send_down, send_up, send_pair, prompt,
        candidate_adapter,
    )
    return totals(all_ids, back, back_pair)


def solution(mesh):
    placed = (
        P("prompt", "wide", None),
        P("prompt", "wide", None),
        P("prompt", "wide", None),
        P("prompt", "wide", None),
        P("prompt", None),
        P("prompt", "wide"),
        P(None, None, None, "wide"),
        P(None, None, None, "wide"),
        P(None, None, None, "wide"),
        P("prompt", "wide", None),
        P("prompt", "wide", None),
    )
    return jax.shard_map(
        functools.partial(body, mesh.shape["prompt"], mesh.shape["wide"]),
        mesh=mesh,
        in_specs=placed,
        out_specs=(
            P(None, None, None, "wide"),
            P(None, None, None, "wide"),
            P(None, None, None, "wide"),
        ),
        check_vma=False,
    )
```
